32 devices in a mesh: dom: 4 (over z), sub: 8 (over y, x, core).
Axes of the slice: x: 2, y: 2, z: 4, core: 2. Of those that a mesh axis runs over, the one named last changes fastest.
Arguments:
- coefficients: float32 [9, 56, 4096], P(None, None, ('dom', 'sub')), may hold values from -6 to 6
- stiffness: float32 [3, 56, 56], replicated, may hold values from -0.75 to 0.75
- jacobians: float32 [3, 9, 9, 4096], P(None, None, None, ('dom', 'sub')), may hold values from -1.25 to 1.25
- face_proj: float32 [4, 21, 56], replicated, may hold values from -0.75 to 0.75
- neigh_proj: float32 [12, 21, 56], replicated, may hold values from -0.75 to 0.75
- lifting: float32 [4, 56, 21], replicated, may hold values from -1.25 to 1.25
- flux_local: float32 [4, 9, 9, 4096], P(None, None, None, ('dom', 'sub')), may hold values from -2 to 2
- flux_neigh: float32 [4, 9, 9, 4096], P(None, None, None, ('dom', 'sub')), may hold values from -2 to 2
- clusters: int32 [4096], P(('dom', 'sub')), may hold values from 0 to 2
- face_slots: int32 [4, 4096], P(None, ('dom', 'sub')), may hold values from 0 to 192, as said below
- orientation: int32 [4, 4096], P(None, ('dom', 'sub')), may hold values from 0 to 11
- send_list: int32 [4, 512], P(None, ('dom', 'sub')), may hold values from 0 to 127, as said below
Outputs:
- increment: float32 [9, 56, 4096], P(None, None, ('dom', 'sub'))
The draws below stay inside these ranges and needn't reach their ends.
Inputs may be any that keep to these rules, and one draw needn't show every extreme that they name: `face_slots`: A face refers to another local element (entry below 128, never the element itself), to a received element, or to the last entry (no neighbour). Every received entry of a neighbour that exists is referred to by exactly one face of the partition; entries of neighbours that do not exist are never referred to. `send_list`: the 16 entries of one row of one partition are distinct local element numbers.
All inputs are finite; a program needn't handle non-finite values.
Results may differ from the reference program's by a relative error of at most 0.0003.
Values sent between devices are 32-bit elements; how exact they have to be, the bound alone decides.
No kernel may reach another device: no remote copies, remote signals or barrier semaphores. Data moves between devices by JAX's collectives and lax.ppermute only.
A program may use at most 192 MiB of HBM per device.

```python
import math
import jax
import jax.numpy as jnp
from jax import lax

FIELDS = 9
BASIS = 56
FACE_BASIS = 21
ORDER = 6
ORIENTS = 12
SUBSTEPS = 4
E_DEV = 128
BSEND = 16
GROUPS = 4
SUBS = 8
PARTITIONS = 32
ELEMS = 4096


def draw_face_slots(key, part):

    def draw_device(device):
        device_key = jax.random.fold_in(key, device)
        key_local, key_rim, key_cross = jax.random.split(device_key, 3)
        positions = jnp.arange(E_DEV, dtype=jnp.int32)[None, :]
        local_slot = (positions + 1 + jax.random.randint(key_local, (4, E_DEV), 0, E_DEV - 1)) % E_DEV
        rim_mask = jax.random.randint(key_rim, (4, E_DEV), 0, 16) == 0
        slots_flat = jnp.where(rim_mask, E_DEV + 4 * BSEND, local_slot).reshape(-1).astype(jnp.int32)
        chosen = jax.random.permutation(key_cross, 4 * E_DEV)[:4 * BSEND]
        sub_pos = device % SUBS
        group_pos = device // SUBS
        direction = jnp.arange(4 * BSEND, dtype=jnp.int32) // BSEND
        has_peer = jnp.where(direction == 0, sub_pos > 0, jnp.where(direction == 1, sub_pos < SUBS - 1, jnp.where(direction == 2, group_pos > 0, group_pos < GROUPS - 1)))
        cross_slot = jnp.where(has_peer, E_DEV + jnp.arange(4 * BSEND, dtype=jnp.int32), E_DEV + 4 * BSEND).astype(jnp.int32)
        slots_flat = slots_flat.at[chosen].set(cross_slot)
        return slots_flat.reshape(4, E_DEV)
    per_device = jax.vmap(draw_device)(jnp.arange(PARTITIONS, dtype=jnp.int32))
    return jnp.moveaxis(per_device, 0, 1).reshape(4, PARTITIONS * E_DEV).astype(jnp.int32)


def draw_send_list(key, part):

    def draw_device(device):
        device_key = jax.random.fold_in(key, device + 7919)
        row_keys = jax.random.split(device_key, 4)
        rows_list = [jax.random.permutation(row_keys[index], E_DEV)[:BSEND] for index in range(4)]
        return jnp.stack(rows_list).astype(jnp.int32)
    per_device = jax.vmap(draw_device)(jnp.arange(PARTITIONS, dtype=jnp.int32))
    return jnp.moveaxis(per_device, 0, 1).reshape(4, PARTITIONS * BSEND).astype(jnp.int32)


def set_ends(values, stream_key, low, high):
    spot = [jax.random.randint(jax.random.fold_in(stream_key, axis), (), 0, length) for axis, length in enumerate(values.shape)]
    widest = values.shape.index(max(values.shape))
    beside = spot[:widest] + [(spot[widest] + 1) % values.shape[widest]] + spot[widest + 1:]
    return values.at[tuple(spot)].set(low).at[tuple(beside)].set(high)


def block_levels(rng, extent, cuts, smallest, largest):
    level, own = 1.0, jax.random.fold_in(rng, 6)
    for axis_at, blocks in cuts:
        draws = jnp.exp(jax.random.uniform(jax.random.fold_in(own, axis_at), (blocks,), jnp.float32, smallest / len(cuts), largest / len(cuts)))
        level = level * jnp.repeat(draws, extent[axis_at] // blocks).reshape([-1 if axis == axis_at else 1 for axis in range(len(extent))])
    return level


def centred(rng, shape, width, reach, cuts=(), kind=jnp.bfloat16):
    drawn = jax.random.normal(rng, shape, jnp.float32) * width
    if len(cuts) > 0:
        drawn = block_levels(rng, shape, cuts, -0.22, 0.18) * drawn
    return jnp.clip(drawn, min=-reach, max=reach).astype(kind)


def setup_inputs(seed: int = 0) -> dict:
    key_of = jax.random.split(jax.random.key(seed), 13)
    return {
        "coefficients": centred(key_of[0], (FIELDS, BASIS, ELEMS), 1.0, 6.0, ((2, 32),), jnp.float32),
        "stiffness": centred(key_of[1], (3, BASIS, BASIS), BASIS ** -0.5, 0.75, (), jnp.float32),
        "jacobians": centred(key_of[2], (3, FIELDS, FIELDS, ELEMS), (3 * FIELDS) ** -0.5, 1.25, ((3, 32),), jnp.float32),
        "face_proj": centred(key_of[3], (4, FACE_BASIS, BASIS), BASIS ** -0.5, 0.75, (), jnp.float32),
        "neigh_proj": centred(key_of[4], (ORIENTS, FACE_BASIS, BASIS), BASIS ** -0.5, 0.75, (), jnp.float32),
        "lifting": centred(key_of[5], (4, BASIS, FACE_BASIS), FACE_BASIS ** -0.5, 1.25, (), jnp.float32),
        "flux_local": centred(key_of[6], (4, FIELDS, FIELDS, ELEMS), FIELDS ** -0.5, 2.0, ((3, 32),), jnp.float32),
        "flux_neigh": centred(key_of[7], (4, FIELDS, FIELDS, ELEMS), FIELDS ** -0.5, 2.0, ((3, 32),), jnp.float32),
        "clusters": set_ends(jax.random.randint(key_of[8], (ELEMS,), 0, 3), jax.random.fold_in(key_of[8], 1), 0, 2).astype(jnp.int32),
        "face_slots": draw_face_slots(jax.random.fold_in(key_of[12], 71), 0),
        "orientation": set_ends(jax.random.randint(key_of[10], (4, ELEMS), 0, ORIENTS), jax.random.fold_in(key_of[10], 1), 0, ORIENTS - 1).astype(jnp.int32),
        "send_list": draw_send_list(jax.random.fold_in(key_of[12], 71), 0),
    }


HIGHEST = lax.Precision.HIGHEST
STEP_LENGTH = 0.5


def derivatives(values, jacobians, stiffness):
    result = [values]
    current = values
    for degree in range(ORDER - 1):
        spatial = jnp.einsum("dab,qbe->dqae", stiffness, current, precision=HIGHEST)
        current = -jnp.einsum("dpqe,dqae->pae", jacobians, spatial, precision=HIGHEST)
        result.append(current)
    return result


def integrate(series, lower_time, upper_time):
    summed = jnp.zeros_like(series[0])
    for degree in range(ORDER):
        weight = (upper_time ** (degree + 1) - lower_time ** (degree + 1)) / math.factorial(degree + 1)
        summed = summed + series[degree] * weight
    return summed


def windows(clusters, substep):
    length = jnp.where(clusters == 0, 1, jnp.where(clusters == 1, 2, 4)).astype(jnp.int32)
    phase_index = substep % length
    lower_time = phase_index.astype(jnp.float32) * STEP_LENGTH
    finished = (substep + 1) % length == 0
    return lower_time, lower_time + STEP_LENGTH, finished


def contribution(own_part, neighbours, jacobians, flux_local, flux_neigh, orientation, stiffness, face_proj, neigh_proj, lifting):
    volume = jnp.einsum("dba,qbe->dqae", stiffness, own_part, precision=HIGHEST)
    volume = jnp.einsum("dpqe,dqae->pae", jacobians, volume, precision=HIGHEST)
    traces = jnp.einsum("fcb,qbe->fqce", face_proj, own_part, precision=HIGHEST)
    local_flux = jnp.einsum("fpqe,fqce->fpce", flux_local, traces, precision=HIGHEST)
    local_term = jnp.einsum("fac,fpce->pae", lifting, local_flux, precision=HIGHEST)
    matrices = neigh_proj[orientation]
    outer_trace = jnp.einsum("fecb,qbfe->fqce", matrices, neighbours, precision=HIGHEST)
    neigh_flux = jnp.einsum("fpqe,fqce->fpce", flux_neigh, outer_trace, precision=HIGHEST)
    neigh_term = jnp.einsum("fac,fpce->pae", lifting, neigh_flux, precision=HIGHEST)
    return volume - local_term - neigh_term


def neighbour_table(face_slots, send_list):
    element = jnp.arange(ELEMS, dtype=jnp.int32)[None, :]
    device = element // E_DEV
    sub_pos = device % SUBS
    group_pos = device // SUBS
    is_local = face_slots < E_DEV
    is_recv = (face_slots >= E_DEV) & (face_slots < E_DEV + 4 * BSEND)
    relative = jnp.clip(face_slots - E_DEV, 0, 4 * BSEND - 1)
    direction = relative // BSEND
    position = relative % BSEND
    offsets = jnp.array([-1, 1, -SUBS, SUBS], dtype=jnp.int32)[direction]
    source_row = jnp.array([1, 0, 3, 2], dtype=jnp.int32)[direction]
    has_peer = jnp.where(direction == 0, sub_pos > 0, jnp.where(direction == 1, sub_pos < SUBS - 1, jnp.where(direction == 2, group_pos > 0, group_pos < GROUPS - 1)))
    source = jnp.clip(device + offsets, 0, PARTITIONS - 1).astype(jnp.int32)
    sender = send_list[source_row, source * BSEND + position]
    remote = source * E_DEV + sender
    result = jnp.where(is_local, device * E_DEV + face_slots, jnp.where(is_recv & has_peer, remote, ELEMS))
    return result.astype(jnp.int32)


def reference(coefficients, stiffness, jacobians, face_proj, neigh_proj, lifting, flux_local, flux_neigh, clusters, face_slots, orientation, send_list):
    neighbour_ids = neighbour_table(face_slots, send_list)

    def to_blocks(array):
        return jnp.moveaxis(array.reshape(array.shape[:-1] + (PARTITIONS, E_DEV)), -2, 0)

    def from_blocks(array):
        moved = jnp.moveaxis(array, 0, -2)
        return moved.reshape(moved.shape[:-2] + (PARTITIONS * E_DEV,))

    jacobian_blocks = to_blocks(jacobians)
    local_blocks = to_blocks(flux_local)
    neigh_blocks = to_blocks(flux_neigh)
    orient_blocks = to_blocks(orientation)
    id_blocks = to_blocks(neighbour_ids)
    applied = jnp.zeros_like(coefficients)
    pending = jnp.zeros_like(coefficients)
    for substep in range(SUBSTEPS):
        current = coefficients + applied
        lower_time, upper_time, finished = windows(clusters, substep)

        def predict(operands):
            values, jacobian_part, lower_part, upper_part = operands
            return integrate(derivatives(values, jacobian_part, stiffness), lower_part, upper_part)

        own_part = from_blocks(lax.map(predict, (to_blocks(current), jacobian_blocks, to_blocks(lower_time), to_blocks(upper_time))))
        padded = jnp.concatenate([own_part, jnp.zeros((FIELDS, BASIS, 1), own_part.dtype)], axis=2)

        def update(operands):
            own_block, id_block, jacobian_part, local_part, neigh_part, orient_part = operands
            neighbours = padded[:, :, id_block]
            return contribution(own_block, neighbours, jacobian_part, local_part, neigh_part, orient_part, stiffness, face_proj, neigh_proj, lifting)

        change = from_blocks(lax.map(update, (to_blocks(own_part), id_blocks, jacobian_blocks, local_blocks, neigh_blocks, orient_blocks)))
        pending = pending + change
        applied = applied + jnp.where(finished, pending, 0.0)
        pending = jnp.where(finished, 0.0, pending)
    return applied
```

```python
import functools
import math

import jax
import jax.numpy as jnp
from jax import lax
from jax.experimental import pallas as pl
from jax.experimental.pallas import tpu as pltpu
from jax.sharding import PartitionSpec as P

ORDER = 6
ORIENTS = 12
FACES = 4
SUBSTEPS = 4
STEP_LENGTH = 0.5
GROUPS = (5, 4)
AXES = ("dom", "sub")


def swaps(doms, subs, axis, phase):
    partner = {}
    for dom in range(doms):
        for sub in range(subs):
            place = sub if axis == "sub" else dom
            count = subs if axis == "sub" else doms
            other = place + 1 if (place - phase) % 2 == 0 else place - 1
            if 0 <= other < count:
                there = (dom, other) if axis == "sub" else (other, sub)
                partner[(dom, sub)] = there
    idle = [(d, s) for d in range(doms) for s in range(subs) if (d, s) not in partner]
    for dom, sub in idle:
        for there in ((dom, sub ^ 1), (dom ^ 1, sub)):
            if (dom, sub) not in partner and there in idle and there not in partner:
                partner[(dom, sub)] = there
                partner[there] = (dom, sub)
    return [
        (dom * subs + sub, there[0] * subs + there[1])
        for (dom, sub), there in sorted(partner.items())
    ]


def rounded(values):
    return values.astype(jnp.bfloat16).astype(jnp.float32)


def stacked(values):
    high = rounded(values)
    low = values - high
    pad = jnp.zeros((8, values.shape[1]), jnp.float32)
    return jnp.concatenate([high, low, high, pad], axis=0).astype(jnp.bfloat16)


def widened(weights):
    high = rounded(weights)
    low = weights - high
    pad = jnp.zeros((weights.shape[0], 8), jnp.float32)
    return jnp.concatenate([high, high, low, pad], axis=1).astype(jnp.bfloat16)


def product(left, right):
    return jnp.dot(left, right, preferred_element_type=jnp.float32)


def directions():
    sub_odd = lax.axis_index("sub") % 2
    dom_odd = lax.axis_index("dom") % 2
    return [1 - sub_odd, sub_odd, 3 - dom_odd, 2 + dom_odd]


def time_phase(clusters, substep):
    phases = [substep % 1, substep % 2, substep % 4]
    ends = [True, (substep + 1) % 2 == 0, (substep + 1) % 4 == 0]
    phase = jnp.where(
        clusters == 0, float(phases[0]), jnp.where(clusters == 1, float(phases[1]), float(phases[2]))
    )
    done = jnp.where(
        clusters == 0, float(ends[0]), jnp.where(clusters == 1, float(ends[1]), float(ends[2]))
    )
    return phase, done


def taylor_weights(clusters, substep):
    phase, _ = time_phase(clusters, substep)
    lower = phase * STEP_LENGTH
    upper = lower + STEP_LENGTH
    weights, low_power, high_power = [], lower, upper
    for degree in range(ORDER):
        weights.append((high_power - low_power) * (1.0 / math.factorial(degree + 1)))
        low_power, high_power = low_power * lower, high_power * upper
    return weights


def series(current, jac, stiff, weights, own, first, second):
    fields, basis, cells = own.shape

    def spatial(target, start, values):
        columns = jnp.concatenate([stacked(value) for value in values], axis=1)
        target[:, start * cells : (start + len(values)) * cells] = product(stiff[...], columns)

    start = 0
    for size in GROUPS:
        values = [current(start + i) for i in range(size)]
        for i in range(size):
            own[start + i] = values[i] * weights[0]
        spatial(first, start, values)
        start += size
    source, target = first, second
    for degree in range(1, ORDER):
        start = 0
        for size in GROUPS:
            total = [None] * size
            for direction in range(3):
                for inner in range(fields):
                    value = source[
                        direction * basis : (direction + 1) * basis,
                        inner * cells : (inner + 1) * cells,
                    ]
                    for i in range(size):
                        term = jac[direction, start + i, pl.ds(inner, 1), :] * value
                        total[i] = term if total[i] is None else total[i] + term
            for i in range(size):
                own[start + i] += total[i] * weights[degree]
            if degree < ORDER - 1:
                spatial(target, start, total)
            start += size
        source, target = target, source


def pack(own, picks, messages):
    fields, basis, cells = own.shape
    rows = own[...].reshape(fields * basis, cells)
    high = rows.astype(jnp.bfloat16)
    low = (rows - high.astype(jnp.float32)).astype(jnp.bfloat16)
    picked = product(jnp.concatenate([high, low], axis=1), picks[...])
    entries = cells // (fields - 1)
    lane = lax.broadcasted_iota(jnp.int32, (1, cells), 1) // entries
    for exchange, message in enumerate(messages):
        columns = slice(exchange * cells, (exchange + 1) * cells)
        main = picked[0:basis, columns]
        for field in range(1, fields - 1):
            main = jnp.where(lane == field, picked[field * basis : (field + 1) * basis, columns], main)
        message[0:basis, :] = main
        last = (fields - 1) * basis
        rest = picked[last : last + 8, columns]
        for tile in range(1, basis // 8):
            rest = jnp.where(
                lane == tile, picked[last + tile * 8 : last + tile * 8 + 8, columns], rest
            )
        message[basis : basis + 8, :] = rest


def start_kernel(
    coefficients, jac, stiffness, clusters, sends,
    own, message_0, message_1, message_2, message_3, stiff, picks,
    first, second,
):
    fields, basis, cells = own.shape
    stiff[...] = widened(-stiffness[...].reshape(3 * basis, basis))
    entries = sends.shape[1]
    rows = directions()
    places = []
    for row in rows:
        entry_row = sends[pl.ds(row, 1), :]
        places += [entry_row] * (cells // entries)
    place = jnp.concatenate(places, axis=1)
    element = lax.broadcasted_iota(jnp.int32, (cells, place.shape[1]), 0)
    hot = jnp.where(element == place, 1.0, 0.0).astype(jnp.bfloat16)
    picks[0:cells, :] = hot
    picks[cells : 2 * cells, :] = hot
    weights = taylor_weights(clusters[...], 0)
    series(lambda field: coefficients[field], jac, stiff, weights, own, first, second)
    pack(own, picks, (message_0, message_1, message_2, message_3))


def local_kernel(own, jac, flux_local, matrices, local_hot, volume, local_flux, traces, spatial):
    fields, basis, cells = own.shape
    wide = traces.shape[0] // fields
    columns = jnp.concatenate([stacked(own[field]) for field in range(fields)], axis=1)
    spatial[...] = product(matrices[...], columns)
    start = 0
    for size in GROUPS:
        total = [None] * size
        for direction in range(3):
            for inner in range(fields):
                value = spatial[
                    direction * basis : (direction + 1) * basis,
                    inner * cells : (inner + 1) * cells,
                ]
                for i in range(size):
                    term = jac[direction, start + i, pl.ds(inner, 1), :] * value
                    total[i] = term if total[i] is None else total[i] + term
        for i in range(size):
            volume[start + i] = total[i]
        start += size
    base = 3 * basis
    for face in range(FACES):
        total = [None] * fields
        for inner in range(fields):
            value = spatial[
                base + face * wide : base + (face + 1) * wide, inner * cells : (inner + 1) * cells
            ]
            for outer in range(fields):
                term = flux_local[face, outer, pl.ds(inner, 1), :] * value
                total[outer] = term if total[outer] is None else total[outer] + term
        for outer in range(fields):
            local_flux[face, outer] = total[outer]
    base += FACES * wide
    highs, lows = [], []
    for pair in range(ORIENTS):
        rows = slice(base + pair * wide, base + (pair + 1) * wide)
        values = jnp.concatenate(
            [spatial[rows, field * cells : (field + 1) * cells] for field in range(fields)], axis=0
        )
        high = rounded(values)
        highs.append(high)
        lows.append(values - high)
    left = jnp.concatenate(
        [jnp.concatenate(highs, axis=1), jnp.concatenate(lows, axis=1)], axis=0
    ).astype(jnp.bfloat16)
    both = product(left, local_hot[...])
    half = fields * wide
    traces[...] = both[:half] + both[half:]


def first_local_kernel(
    own, jac, flux_local, stiffness, face_proj, neigh_proj, lifting, slots, orientation,
    volume, local_flux, traces, matrices, local_hot, halo_hot, halo_pairs, lift,
    spatial, plain,
):
    fields, basis, cells = own.shape
    face_basis = face_proj.shape[1]
    wide = traces.shape[0] // fields
    plain[...] = jnp.zeros_like(plain)
    for direction in range(3):
        plain[direction * basis : (direction + 1) * basis, :] = stiffness[direction].T
    row = 3 * basis
    for face in range(FACES):
        plain[row : row + face_basis, :] = face_proj[face]
        row += wide
    for pair in range(ORIENTS):
        plain[row : row + face_basis, :] = neigh_proj[pair]
        row += wide
    matrices[...] = widened(plain[...])
    empty = jnp.zeros((basis, wide - face_basis), jnp.float32)
    parts = []
    for face in range(FACES):
        parts += [lifting[face], empty]
    lift_plain = jnp.concatenate(parts, axis=1)
    lift_high = rounded(lift_plain)
    lift[...] = jnp.concatenate([lift_high, lift_high, lift_plain - lift_high], axis=1).astype(
        jnp.bfloat16
    )
    slot_row = jnp.concatenate([slots[face : face + 1, :] for face in range(FACES)], axis=1)
    pair_row = jnp.concatenate([orientation[face : face + 1, :] for face in range(FACES)], axis=1)
    element = lax.broadcasted_iota(jnp.int32, (cells, FACES * cells), 0)
    hit = jnp.where(element == slot_row, pair_row, -1)
    for pair in range(ORIENTS):
        local_hot[pair * cells : (pair + 1) * cells, :] = jnp.where(hit == pair, 1.0, 0.0).astype(
            jnp.bfloat16
        )
    entries = cells // (fields - 1)
    rows = directions()
    keys = [cells + row * entries for row in rows]
    entry = lax.broadcasted_iota(jnp.int32, (cells, 1), 0)
    for exchange in range(4):
        key = keys[exchange] + entry % entries
        halo_hot[exchange * cells : (exchange + 1) * cells, :] = jnp.where(
            slot_row == key, 1.0, 0.0
        ).astype(jnp.bfloat16)
    key = jnp.full((cells, 1), -1, jnp.int32)
    for exchange in range(4):
        key = jnp.where(entry // entries == exchange, keys[exchange] + entry % entries, key)
    halo_hot[4 * cells : 5 * cells, :] = jnp.where(slot_row == key, 1.0, 0.0).astype(jnp.bfloat16)
    pair_rows = jnp.broadcast_to(pair_row.astype(jnp.float32), (8, FACES * cells))
    halo_pairs[...] = lax.dot_general(
        pair_rows.astype(jnp.bfloat16),
        halo_hot[...],
        (((1,), (1,)), ((), ())),
        preferred_element_type=jnp.float32,
    )
    local_kernel(own, jac, flux_local, matrices, local_hot, volume, local_flux, traces, spatial)


def remote_part(messages, matrices, halo_hot, halo_pairs, traces):
    cells = messages[0].shape[1]
    basis = messages[0].shape[0] - 8
    half = traces.shape[0]
    wide = (matrices.shape[0] - 3 * basis) // (FACES + ORIENTS)
    fields = half // wide
    entries = cells // (fields - 1)
    lane = lax.broadcasted_iota(jnp.int32, (1, cells), 1) // entries
    last = []
    for tile in range(basis // 8):
        total = jnp.zeros((8, cells), jnp.float32)
        for exchange in range(4):
            value = messages[exchange][basis : basis + 8, :]
            shift = ((exchange - tile) * entries) % cells
            if shift:
                value = pltpu.roll(value, shift, 1)
            total = jnp.where(lane == exchange, value, total)
        last.append(total)
    parts = [message[0:basis, :] for message in messages] + [jnp.concatenate(last, axis=0)]
    columns = jnp.concatenate([stacked(part) for part in parts], axis=1)
    base = 3 * basis + FACES * wide
    projected = product(matrices[base:, :], columns)
    pair_row = halo_pairs[0:1, :]
    chosen = projected[0:wide, :]
    for pair in range(1, ORIENTS):
        chosen = jnp.where(
            pair_row == float(pair), projected[pair * wide : (pair + 1) * wide, :], chosen
        )
    high = rounded(chosen)
    low = chosen - high
    left = []
    for part in (high, low):
        for field in range(fields - 1):
            left.append(
                jnp.concatenate(
                    [
                        jnp.where(lane == field, part[:, c * cells : (c + 1) * cells], 0.0)
                        for c in range(4)
                    ],
                    axis=1,
                )
            )
    most = (fields - 1) * wide
    both = product(jnp.concatenate(left, axis=0).astype(jnp.bfloat16), halo_hot[0 : 4 * cells, :])
    tail = jnp.concatenate([high[:, 4 * cells :], low[:, 4 * cells :]], axis=0)
    both_tail = product(tail.astype(jnp.bfloat16), halo_hot[4 * cells :, :])
    return (
        traces[0:most, :] + both[:most] + both[most:],
        traces[most:, :] + both_tail[:wide] + both_tail[wide:],
    )


def change(remote, volume, local_flux, flux_neigh, lift):
    main, tail = remote
    fields, _, cells = volume.shape
    wide = local_flux.shape[2]
    rows = []
    for face in range(FACES):
        total = [local_flux[face, outer] for outer in range(fields)]
        for inner in range(fields):
            source = main[inner * wide : (inner + 1) * wide] if inner < fields - 1 else tail
            value = source[:, face * cells : (face + 1) * cells]
            for outer in range(fields):
                total[outer] = total[outer] + flux_neigh[face, outer, pl.ds(inner, 1), :] * value
        rows.append(jnp.concatenate(total, axis=1))
    flux = jnp.concatenate(rows, axis=0)
    high = rounded(flux)
    right = jnp.concatenate([high, flux - high, high], axis=0).astype(jnp.bfloat16)
    lifted = product(lift[...], right)
    return [volume[p] - lifted[:, p * cells : (p + 1) * cells] for p in range(fields)]


def step_kernel(
    substep,
    coefficients, applied_in, pending_in, jac, stiff, clusters, picks,
    in_0, in_1, in_2, in_3,
    volume, local_flux, traces, flux_neigh, matrices, halo_hot, halo_pairs, lift,
    applied, pending, own, message_0, message_1, message_2, message_3,
    first, second,
):
    fields = volume.shape[0]
    remote = remote_part((in_0, in_1, in_2, in_3), matrices, halo_hot, halo_pairs, traces)
    updates = change(remote, volume, local_flux, flux_neigh, lift)
    _, done = time_phase(clusters[...], substep)
    finished = done > 0.5
    for field in range(fields):
        waiting = updates[field]
        if substep > 0:
            waiting = waiting + pending_in[field]
        passed = jnp.where(finished, waiting, 0.0)
        applied[field] = passed + applied_in[field] if substep > 0 else passed
        pending[field] = jnp.where(finished, 0.0, waiting)
    weights = taylor_weights(clusters[...], substep + 1)
    series(
        lambda field: coefficients[field] + applied[field], jac, stiff, weights, own, first, second
    )
    pack(own, picks, (message_0, message_1, message_2, message_3))


def last_kernel(
    applied_in, pending_in,
    in_0, in_1, in_2, in_3,
    volume, local_flux, traces, flux_neigh, matrices, halo_hot, halo_pairs, lift,
    increment,
):
    remote = remote_part((in_0, in_1, in_2, in_3), matrices, halo_hot, halo_pairs, traces)
    updates = change(remote, volume, local_flux, flux_neigh, lift)
    for field in range(volume.shape[0]):
        increment[field] = applied_in[field] + (pending_in[field] + updates[field])


def call(kernel, outs, scratch, flops, *operands):
    block = pl.BlockSpec(memory_space=pltpu.VMEM)
    return pl.pallas_call(
        kernel,
        out_shape=outs,
        in_specs=[block] * len(operands),
        out_specs=[block] * len(outs),
        scratch_shapes=[pltpu.VMEM(shape, jnp.float32) for shape in scratch],
        compiler_params=pltpu.CompilerParams(vmem_limit_bytes=40 << 20),
        cost_estimate=pl.CostEstimate(flops=flops, bytes_accessed=1 << 20, transcendentals=0),
    )(*operands)


def on_device(
    coefficients, stiffness, jacobians, face_proj, neigh_proj, lifting,
    flux_local, flux_neigh, clusters, face_slots, orientation, send_list, *, doms, subs,
):
    fields, basis, cells = coefficients.shape
    wide = -(-face_proj.shape[1] // 8) * 8
    clusters = clusters.reshape(1, cells)
    exchanges = [
        swaps(doms, subs, axis, phase) for axis in ("sub", "dom") for phase in (0, 1)
    ]

    def f32(*shape):
        return jax.ShapeDtypeStruct(shape, jnp.float32)

    def bf16(*shape):
        return jax.ShapeDtypeStruct(shape, jnp.bfloat16)

    state = f32(fields, basis, cells)
    message = f32(basis + 8, cells)
    depth = 3 * basis + 8
    rows = 3 * basis + (FACES + ORIENTS) * wide
    derived = (3 * basis, fields * cells)
    faces = FACES * cells

    def exchange(messages):
        return [lax.ppermute(m, AXES, pairs) for m, pairs in zip(messages, exchanges)]

    own, *messages, stiff, picks = call(
        start_kernel,
        [state] + [message] * 4 + [bf16(3 * basis, depth), bf16(2 * cells, 4 * cells)],
        [derived, derived], 1 << 27,
        coefficients, jacobians, stiffness, clusters, send_list,
    )
    local_outs = [state, f32(FACES, fields, wide, cells), f32(fields * wide, faces)]
    applied = pending = coefficients
    for substep in range(SUBSTEPS):
        received = exchange(messages)
        if substep == 0:
            volume, local_flux, traces, matrices, local_hot, halo_hot, halo_pairs, lift = call(
                first_local_kernel,
                local_outs
                + [
                    bf16(rows, depth), bf16(ORIENTS * cells, faces), bf16(5 * cells, faces),
                    f32(8, 5 * cells), bf16(basis, 3 * FACES * wide),
                ],
                [(rows, fields * cells), (rows, basis)], 1 << 27,
                own, jacobians, flux_local, stiffness, face_proj, neigh_proj, lifting,
                face_slots, orientation,
            )
        else:
            volume, local_flux, traces = call(
                local_kernel, local_outs, [(rows, fields * cells)], 1 << 27,
                own, jacobians, flux_local, matrices, local_hot,
            )
        rest = (
            *received, volume, local_flux, traces, flux_neigh, matrices, halo_hot, halo_pairs, lift,
        )
        if substep < SUBSTEPS - 1:
            applied, pending, own, *messages = call(
                functools.partial(step_kernel, substep),
                [state] * 3 + [message] * 4, [derived, derived], 1 << 27,
                coefficients, applied, pending, jacobians, stiff, clusters, picks, *rest,
            )
        else:
            (increment,) = call(last_kernel, [state], [], 1 << 27, applied, pending, *rest)
    return increment


def solution(mesh):
    split = ("dom", "sub")
    placed = (
        P(None, None, split), P(), P(None, None, None, split), P(), P(), P(),
        P(None, None, None, split), P(None, None, None, split), P(split),
        P(None, split), P(None, split), P(None, split),
    )
    return jax.shard_map(
        functools.partial(on_device, doms=mesh.shape["dom"], subs=mesh.shape["sub"]),
        mesh=mesh,
        in_specs=placed,
        out_specs=P(None, None, split),
        check_vma=False,
    )
```

```python
import functools
import math

import jax
import jax.numpy as jnp
from jax import lax
from jax.experimental import pallas as pl
from jax.experimental.pallas import tpu as pltpu
from jax.sharding import PartitionSpec as P

ORDER = 6
ORIENTS = 12
FACES = 4
SUBSTEPS = 4
STEP_LENGTH = 0.5
GROUPS = (5, 4)
AXES = ("dom", "sub")


def swaps(doms, subs, axis, phase):
    partner = {}
    for dom in range(doms):
        for sub in range(subs):
            place = sub if axis == "sub" else dom
            count = subs if axis == "sub" else doms
            other = place + 1 if (place - phase) % 2 == 0 else place - 1
            if 0 <= other < count:
                there = (dom, other) if axis == "sub" else (other, sub)
                partner[(dom, sub)] = there
    idle = [(d, s) for d in range(doms) for s in range(subs) if (d, s) not in partner]
    for dom, sub in idle:
        for there in ((dom, sub ^ 1), (dom ^ 1, sub)):
            if (dom, sub) not in partner and there in idle and there not in partner:
                partner[(dom, sub)] = there
                partner[there] = (dom, sub)
    return [
        (dom * subs + sub, there[0] * subs + there[1])
        for (dom, sub), there in sorted(partner.items())
    ]


def rounded(values):
    return values.astype(jnp.bfloat16).astype(jnp.float32)


def stacked(values):
    high = rounded(values)
    low = values - high
    pad = jnp.zeros((8, values.shape[1]), jnp.float32)
    return jnp.concatenate([high, low, high, pad], axis=0).astype(jnp.bfloat16)


def widened(weights):
    high = rounded(weights)
    low = weights - high
    pad = jnp.zeros((weights.shape[0], 8), jnp.float32)
    return jnp.concatenate([high, high, low, pad], axis=1).astype(jnp.bfloat16)


def product(left, right):
    return jnp.dot(left, right, preferred_element_type=jnp.float32)


def directions():
    sub_odd = lax.axis_index("sub") % 2
    dom_odd = lax.axis_index("dom") % 2
    return [1 - sub_odd, sub_odd, 3 - dom_odd, 2 + dom_odd]


def time_phase(clusters, substep):
    phases = [substep % 1, substep % 2, substep % 4]
    ends = [True, (substep + 1) % 2 == 0, (substep + 1) % 4 == 0]
    phase = jnp.where(
        clusters == 0, float(phases[0]), jnp.where(clusters == 1, float(phases[1]), float(phases[2]))
    )
    done = jnp.where(
        clusters == 0, float(ends[0]), jnp.where(clusters == 1, float(ends[1]), float(ends[2]))
    )
    return phase, done


def taylor_weights(clusters, substep):
    phase, _ = time_phase(clusters, substep)
    lower = phase * STEP_LENGTH
    upper = lower + STEP_LENGTH
    weights, low_power, high_power = [], lower, upper
    for degree in range(ORDER):
        weights.append((high_power - low_power) * (1.0 / math.factorial(degree + 1)))
        low_power, high_power = low_power * lower, high_power * upper
    return weights


def series(current, jac, stiff, weights, own, first, second):
    fields, basis, cells = own.shape

    def spatial(target, start, values):
        columns = jnp.concatenate([stacked(value) for value in values], axis=1)
        target[:, start * cells : (start + len(values)) * cells] = product(stiff[...], columns)

    start = 0
    for size in GROUPS:
        values = [current(start + i) for i in range(size)]
        for i in range(size):
            own[start + i] = values[i] * weights[0]
        spatial(first, start, values)
        start += size
    source, target = first, second
    for degree in range(1, ORDER):
        start = 0
        for size in GROUPS:
            total = [None] * size
            for direction in range(3):
                for inner in range(fields):
                    value = source[
                        direction * basis : (direction + 1) * basis,
                        inner * cells : (inner + 1) * cells,
                    ]
                    for i in range(size):
                        term = jac[start + i, inner, pl.ds(direction, 1), :] * value
                        total[i] = term if total[i] is None else total[i] + term
            for i in range(size):
                own[start + i] += total[i] * weights[degree]
            if degree < ORDER - 1:
                spatial(target, start, total)
            start += size
        source, target = target, source


def pack(own, picks, messages):
    fields, basis, cells = own.shape
    rows = own[...].reshape(fields * basis, cells)
    high = rows.astype(jnp.bfloat16)
    low = (rows - high.astype(jnp.float32)).astype(jnp.bfloat16)
    picked = product(jnp.concatenate([high, low], axis=1), picks[...])
    entries = cells // (fields - 1)
    lane = lax.broadcasted_iota(jnp.int32, (1, cells), 1) // entries
    for exchange, message in enumerate(messages):
        columns = slice(exchange * cells, (exchange + 1) * cells)
        main = picked[0:basis, columns]
        for field in range(1, fields - 1):
            main = jnp.where(lane == field, picked[field * basis : (field + 1) * basis, columns], main)
        message[0:basis, :] = main
        last = (fields - 1) * basis
        rest = picked[last : last + 8, columns]
        for tile in range(1, basis // 8):
            rest = jnp.where(
                lane == tile, picked[last + tile * 8 : last + tile * 8 + 8, columns], rest
            )
        message[basis : basis + 8, :] = rest


def start_kernel(
    stiffness_far, sends_far, clusters_far, coefficients_far, jac_far, *rest
):
    far, rest = rest[:7], rest[7:]
    own, message_0, message_1, message_2, message_3, stiff, picks = rest[:7]
    clusters, coefficients, jac, stiffness = rest[7:11]
    near, (first, second, sends, arrived) = rest[11:18], rest[18:]
    fields, basis, cells = own.shape
    pairs = (
        (stiffness_far, stiffness),
        (sends_far, sends),
        (clusters_far, clusters),
        (coefficients_far, coefficients),
        (jac_far, jac),
        *zip(far, near),
    )
    copies = [
        pltpu.make_async_copy(source, target, arrived.at[i])
        for i, (source, target) in enumerate(pairs)
    ]
    for copy in copies:
        copy.start()
    copies[0].wait()
    stiff[...] = widened(-stiffness[...].reshape(3 * basis, basis))
    copies[1].wait()
    entries = sends.shape[1]
    rows = directions()
    places = []
    for row in rows:
        entry_row = sends[pl.ds(row, 1), :]
        places += [entry_row] * (cells // entries)
    place = jnp.concatenate(places, axis=1)
    element = lax.broadcasted_iota(jnp.int32, (cells, place.shape[1]), 0)
    hot = jnp.where(element == place, 1.0, 0.0).astype(jnp.bfloat16)
    picks[0:cells, :] = hot
    picks[cells : 2 * cells, :] = hot
    for copy in copies[2:5]:
        copy.wait()
    weights = taylor_weights(clusters[...], 0)
    series(lambda field: coefficients[field], jac, stiff, weights, own, first, second)
    pack(own, picks, (message_0, message_1, message_2, message_3))
    for copy in copies[5:]:
        copy.wait()


def local_kernel(own, jac, flux_local, matrices, local_hot, volume, local_flux, traces, spatial):
    fields, basis, cells = own.shape
    wide = traces.shape[0] // fields
    columns = jnp.concatenate([stacked(own[field]) for field in range(fields)], axis=1)
    spatial[...] = product(matrices[...], columns)
    start = 0
    for size in GROUPS:
        total = [None] * size
        for direction in range(3):
            for inner in range(fields):
                value = spatial[
                    direction * basis : (direction + 1) * basis,
                    inner * cells : (inner + 1) * cells,
                ]
                for i in range(size):
                    term = jac[start + i, inner, pl.ds(direction, 1), :] * value
                    total[i] = term if total[i] is None else total[i] + term
        for i in range(size):
            volume[start + i] = total[i]
        start += size
    base = 3 * basis
    for face in range(FACES):
        total = [None] * fields
        for inner in range(fields):
            value = spatial[
                base + face * wide : base + (face + 1) * wide, inner * cells : (inner + 1) * cells
            ]
            for outer in range(fields):
                term = flux_local[outer, inner, pl.ds(face, 1), :] * value
                total[outer] = term if total[outer] is None else total[outer] + term
        for outer in range(fields):
            local_flux[face, outer] = total[outer]
    base += FACES * wide
    highs, lows = [], []
    for pair in range(ORIENTS):
        rows = slice(base + pair * wide, base + (pair + 1) * wide)
        values = jnp.concatenate(
            [spatial[rows, field * cells : (field + 1) * cells] for field in range(fields)], axis=0
        )
        high = rounded(values)
        highs.append(high)
        lows.append(values - high)
    left = jnp.concatenate(
        [jnp.concatenate(highs, axis=1), jnp.concatenate(lows, axis=1)], axis=0
    ).astype(jnp.bfloat16)
    both = product(left, local_hot[...])
    half = fields * wide
    traces[...] = both[:half] + both[half:]


def first_local_kernel(
    own, jac, flux_local, stiffness, face_proj, neigh_proj, lifting, slots, orientation,
    volume, local_flux, traces, matrices, local_hot, halo_hot, halo_pairs, lift,
    spatial, plain,
):
    fields, basis, cells = own.shape
    face_basis = face_proj.shape[0]
    wide = traces.shape[0] // fields
    plain[...] = jnp.zeros_like(plain)
    for direction in range(3):
        plain[direction * basis : (direction + 1) * basis, :] = stiffness[direction].T
    row = 3 * basis
    for face in range(FACES):
        plain[row : row + face_basis, :] = face_proj[:, face, :]
        row += wide
    for pair in range(ORIENTS):
        plain[row : row + face_basis, :] = neigh_proj[pair]
        row += wide
    matrices[...] = widened(plain[...])
    empty = jnp.zeros((wide - face_basis, basis), jnp.float32)
    parts = []
    for face in range(FACES):
        parts += [lifting[:, face, :], empty]
    lift_plain = jnp.concatenate(parts, axis=0).T
    lift_high = rounded(lift_plain)
    lift[...] = jnp.concatenate([lift_high, lift_high, lift_plain - lift_high], axis=1).astype(
        jnp.bfloat16
    )
    slot_row = jnp.concatenate([slots[face : face + 1, :] for face in range(FACES)], axis=1)
    pair_row = jnp.concatenate([orientation[face : face + 1, :] for face in range(FACES)], axis=1)
    element = lax.broadcasted_iota(jnp.int32, (cells, FACES * cells), 0)
    hit = jnp.where(element == slot_row, pair_row, -1)
    for pair in range(ORIENTS):
        local_hot[pair * cells : (pair + 1) * cells, :] = jnp.where(hit == pair, 1.0, 0.0).astype(
            jnp.bfloat16
        )
    entries = cells // (fields - 1)
    rows = directions()
    keys = [cells + row * entries for row in rows]
    entry = lax.broadcasted_iota(jnp.int32, (cells, 1), 0)
    for exchange in range(4):
        key = keys[exchange] + entry % entries
        halo_hot[exchange * cells : (exchange + 1) * cells, :] = jnp.where(
            slot_row == key, 1.0, 0.0
        ).astype(jnp.bfloat16)
    key = jnp.full((cells, 1), -1, jnp.int32)
    for exchange in range(4):
        key = jnp.where(entry // entries == exchange, keys[exchange] + entry % entries, key)
    halo_hot[4 * cells : 5 * cells, :] = jnp.where(slot_row == key, 1.0, 0.0).astype(jnp.bfloat16)
    pair_rows = jnp.broadcast_to(pair_row.astype(jnp.float32), (8, FACES * cells))
    halo_pairs[...] = lax.dot_general(
        pair_rows.astype(jnp.bfloat16),
        halo_hot[...],
        (((1,), (1,)), ((), ())),
        preferred_element_type=jnp.float32,
    )
    local_kernel(own, jac, flux_local, matrices, local_hot, volume, local_flux, traces, spatial)


def remote_part(messages, matrices, halo_hot, halo_pairs, traces):
    cells = messages[0].shape[1]
    basis = messages[0].shape[0] - 8
    half = traces.shape[0]
    wide = (matrices.shape[0] - 3 * basis) // (FACES + ORIENTS)
    fields = half // wide
    entries = cells // (fields - 1)
    lane = lax.broadcasted_iota(jnp.int32, (1, cells), 1) // entries
    last = []
    for tile in range(basis // 8):
        total = jnp.zeros((8, cells), jnp.float32)
        for exchange in range(4):
            value = messages[exchange][basis : basis + 8, :]
            shift = ((exchange - tile) * entries) % cells
            if shift:
                value = pltpu.roll(value, shift, 1)
            total = jnp.where(lane == exchange, value, total)
        last.append(total)
    parts = [message[0:basis, :] for message in messages] + [jnp.concatenate(last, axis=0)]
    columns = jnp.concatenate([stacked(part) for part in parts], axis=1)
    base = 3 * basis + FACES * wide
    projected = product(matrices[base:, :], columns)
    pair_row = halo_pairs[0:1, :]
    chosen = projected[0:wide, :]
    for pair in range(1, ORIENTS):
        chosen = jnp.where(
            pair_row == float(pair), projected[pair * wide : (pair + 1) * wide, :], chosen
        )
    high = rounded(chosen)
    low = chosen - high
    left = []
    for part in (high, low):
        for field in range(fields - 1):
            left.append(
                jnp.concatenate(
                    [
                        jnp.where(lane == field, part[:, c * cells : (c + 1) * cells], 0.0)
                        for c in range(4)
                    ],
                    axis=1,
                )
            )
    most = (fields - 1) * wide
    both = product(jnp.concatenate(left, axis=0).astype(jnp.bfloat16), halo_hot[0 : 4 * cells, :])
    tail = jnp.concatenate([high[:, 4 * cells :], low[:, 4 * cells :]], axis=0)
    both_tail = product(tail.astype(jnp.bfloat16), halo_hot[4 * cells :, :])
    return (
        traces[0:most, :] + both[:most] + both[most:],
        traces[most:, :] + both_tail[:wide] + both_tail[wide:],
    )


def change(remote, volume, local_flux, flux_neigh, lift):
    main, tail = remote
    fields, _, cells = volume.shape
    wide = local_flux.shape[2]
    rows = []
    for face in range(FACES):
        total = [local_flux[face, outer] for outer in range(fields)]
        for inner in range(fields):
            source = main[inner * wide : (inner + 1) * wide] if inner < fields - 1 else tail
            value = source[:, face * cells : (face + 1) * cells]
            for outer in range(fields):
                total[outer] = total[outer] + flux_neigh[outer, inner, pl.ds(face, 1), :] * value
        rows.append(jnp.concatenate(total, axis=1))
    flux = jnp.concatenate(rows, axis=0)
    high = rounded(flux)
    right = jnp.concatenate([high, flux - high, high], axis=0).astype(jnp.bfloat16)
    lifted = product(lift[...], right)
    return [volume[p] - lifted[:, p * cells : (p + 1) * cells] for p in range(fields)]


def step_kernel(
    substep,
    coefficients, applied_in, pending_in, jac, stiff, clusters, picks,
    in_0, in_1, in_2, in_3,
    volume, local_flux, traces, flux_neigh, matrices, halo_hot, halo_pairs, lift,
    applied, pending, own, message_0, message_1, message_2, message_3,
    first, second,
):
    fields = volume.shape[0]
    remote = remote_part((in_0, in_1, in_2, in_3), matrices, halo_hot, halo_pairs, traces)
    updates = change(remote, volume, local_flux, flux_neigh, lift)
    _, done = time_phase(clusters[...], substep)
    finished = done > 0.5
    for field in range(fields):
        waiting = updates[field]
        if substep > 0:
            waiting = waiting + pending_in[field]
        passed = jnp.where(finished, waiting, 0.0)
        applied[field] = passed + applied_in[field] if substep > 0 else passed
        pending[field] = jnp.where(finished, 0.0, waiting)
    weights = taylor_weights(clusters[...], substep + 1)
    series(
        lambda field: coefficients[field] + applied[field], jac, stiff, weights, own, first, second
    )
    pack(own, picks, (message_0, message_1, message_2, message_3))


def last_kernel(
    applied_in, pending_in,
    in_0, in_1, in_2, in_3,
    volume, local_flux, traces, flux_neigh, matrices, halo_hot, halo_pairs, lift,
    increment,
):
    remote = remote_part((in_0, in_1, in_2, in_3), matrices, halo_hot, halo_pairs, traces)
    updates = change(remote, volume, local_flux, flux_neigh, lift)
    for field in range(volume.shape[0]):
        increment[field] = applied_in[field] + (pending_in[field] + updates[field])


def call(kernel, outs, scratch, flops, *operands, far=False):
    block = pl.BlockSpec(memory_space=pltpu.VMEM)
    source = pl.BlockSpec(memory_space=pltpu.HBM) if far else block
    if far:
        operands = [pltpu.with_memory_space_constraint(x, pltpu.HBM) for x in operands]
    return pl.pallas_call(
        kernel,
        out_shape=outs,
        in_specs=[source] * len(operands),
        out_specs=[block] * len(outs),
        scratch_shapes=scratch,
        compiler_params=pltpu.CompilerParams(vmem_limit_bytes=40 << 20),
        cost_estimate=pl.CostEstimate(flops=flops, bytes_accessed=1 << 20, transcendentals=0),
    )(*operands)


def on_device(
    coefficients, stiffness, jacobians, face_proj, neigh_proj, lifting,
    flux_local, flux_neigh, clusters, face_slots, orientation, send_list, *, doms, subs,
):
    fields, basis, cells = coefficients.shape
    wide = -(-face_proj.shape[1] // 8) * 8
    clusters = clusters.reshape(1, cells)
    jacobians = jnp.transpose(jacobians, (1, 2, 0, 3))
    flux_local = jnp.transpose(flux_local, (1, 2, 0, 3))
    flux_neigh = jnp.transpose(flux_neigh, (1, 2, 0, 3))
    face_proj = jnp.transpose(face_proj, (1, 0, 2))
    lifting = jnp.transpose(lifting, (2, 0, 1))
    exchanges = [
        swaps(doms, subs, axis, phase) for axis in ("sub", "dom") for phase in (0, 1)
    ]

    def f32(*shape):
        return jax.ShapeDtypeStruct(shape, jnp.float32)

    def bf16(*shape):
        return jax.ShapeDtypeStruct(shape, jnp.bfloat16)

    state = f32(fields, basis, cells)
    message = f32(basis + 8, cells)
    depth = 3 * basis + 8
    rows = 3 * basis + (FACES + ORIENTS) * wide
    derived = pltpu.VMEM((3 * basis, fields * cells), jnp.float32)
    faces = FACES * cells

    def exchange(messages):
        return [lax.ppermute(m, AXES, pairs) for m, pairs in zip(messages, exchanges)]

    first = [stiffness, send_list, clusters, coefficients, jacobians]
    later = [flux_local, flux_neigh, face_proj, neigh_proj, lifting, face_slots, orientation]
    near = [clusters, coefficients, jacobians, stiffness, *later]
    own, *given = call(
        start_kernel,
        [state] + [message] * 4 + [bf16(3 * basis, depth), bf16(2 * cells, 4 * cells)]
        + [jax.ShapeDtypeStruct(x.shape, x.dtype) for x in near],
        [
            derived, derived, pltpu.VMEM(send_list.shape, send_list.dtype),
            pltpu.SemaphoreType.DMA((len(first) + len(later),)),
        ],
        1 << 27, *first, *later, far=True,
    )
    messages, (stiff, picks), near = given[:4], given[4:6], given[6:]
    clusters, coefficients, jacobians, stiffness = near[:4]
    flux_local, flux_neigh, face_proj, neigh_proj, lifting, face_slots, orientation = near[4:]
    local_outs = [state, f32(FACES, fields, wide, cells), f32(fields * wide, faces)]
    applied = pending = coefficients
    for substep in range(SUBSTEPS):
        received = exchange(messages)
        if substep == 0:
            volume, local_flux, traces, matrices, local_hot, halo_hot, halo_pairs, lift = call(
                first_local_kernel,
                local_outs
                + [
                    bf16(rows, depth), bf16(ORIENTS * cells, faces), bf16(5 * cells, faces),
                    f32(8, 5 * cells), bf16(basis, 3 * FACES * wide),
                ],
                [pltpu.VMEM((rows, fields * cells), jnp.float32), pltpu.VMEM((rows, basis), jnp.float32)], 1 << 27,
                own, jacobians, flux_local, stiffness, face_proj, neigh_proj, lifting,
                face_slots, orientation,
            )
        else:
            volume, local_flux, traces = call(
                local_kernel, local_outs, [pltpu.VMEM((rows, fields * cells), jnp.float32)], 1 << 27,
                own, jacobians, flux_local, matrices, local_hot,
            )
        rest = (
            *received, volume, local_flux, traces, flux_neigh, matrices, halo_hot, halo_pairs, lift,
        )
        if substep < SUBSTEPS - 1:
            applied, pending, own, *messages = call(
                functools.partial(step_kernel, substep),
                [state] * 3 + [message] * 4, [derived, derived], 1 << 27,
                coefficients, applied, pending, jacobians, stiff, clusters, picks, *rest,
            )
        else:
            (increment,) = call(last_kernel, [state], [], 1 << 27, applied, pending, *rest)
    return increment


def solution(mesh):
    split = ("dom", "sub")
    placed = (
        P(None, None, split), P(), P(None, None, None, split), P(), P(), P(),
        P(None, None, None, split), P(None, None, None, split), P(split),
        P(None, split), P(None, split), P(None, split),
    )
    return jax.shard_map(
        functools.partial(on_device, doms=mesh.shape["dom"], subs=mesh.shape["sub"]),
        mesh=mesh,
        in_specs=placed,
        out_specs=P(None, None, split),
        check_vma=False,
    )
```

```python
import functools
import math

import jax
import jax.numpy as jnp
from jax import lax
from jax.experimental import pallas as pl
from jax.experimental.pallas import tpu as pltpu
from jax.sharding import PartitionSpec as P

ORDER = 6
ORIENTS = 12
FACES = 4
SUBSTEPS = 4
STEP_LENGTH = 0.5
GROUPS = (5, 4)
PAIR_GROUPS = (3, 2)
AXES = ("dom", "sub")


def swaps(doms, subs, axis, phase):
    partner = {}
    for dom in range(doms):
        for sub in range(subs):
            place = sub if axis == "sub" else dom
            count = subs if axis == "sub" else doms
            other = place + 1 if (place - phase) % 2 == 0 else place - 1
            if 0 <= other < count:
                there = (dom, other) if axis == "sub" else (other, sub)
                partner[(dom, sub)] = there
    idle = [(d, s) for d in range(doms) for s in range(subs) if (d, s) not in partner]
    for dom, sub in idle:
        for there in ((dom, sub ^ 1), (dom ^ 1, sub)):
            if (dom, sub) not in partner and there in idle and there not in partner:
                partner[(dom, sub)] = there
                partner[there] = (dom, sub)
    return [
        (dom * subs + sub, there[0] * subs + there[1])
        for (dom, sub), there in sorted(partner.items())
    ]


def rounded(values):
    return values.astype(jnp.bfloat16).astype(jnp.float32)


def stacked(values):
    high = rounded(values)
    low = values - high
    pad = jnp.zeros((8, values.shape[1]), jnp.float32)
    return jnp.concatenate([high, low, high, pad], axis=0).astype(jnp.bfloat16)


def widened(weights):
    high = rounded(weights)
    low = weights - high
    pad = jnp.zeros((weights.shape[0], 8), jnp.float32)
    return jnp.concatenate([high, high, low, pad], axis=1).astype(jnp.bfloat16)


def product(left, right):
    return jnp.dot(left, right, preferred_element_type=jnp.float32)


def directions():
    sub_odd = lax.axis_index("sub") % 2
    dom_odd = lax.axis_index("dom") % 2
    return [1 - sub_odd, sub_odd, 3 - dom_odd, 2 + dom_odd]


def time_phase(clusters, substep):
    phases = [substep % 1, substep % 2, substep % 4]
    ends = [True, (substep + 1) % 2 == 0, (substep + 1) % 4 == 0]
    phase = jnp.where(
        clusters == 0, float(phases[0]), jnp.where(clusters == 1, float(phases[1]), float(phases[2]))
    )
    done = jnp.where(
        clusters == 0, float(ends[0]), jnp.where(clusters == 1, float(ends[1]), float(ends[2]))
    )
    return phase, done


def taylor_weights(clusters, substep):
    phase, _ = time_phase(clusters, substep)
    lower = phase * STEP_LENGTH
    upper = lower + STEP_LENGTH
    weights, low_power, high_power = [], lower, upper
    for degree in range(ORDER):
        weights.append((high_power - low_power) * (1.0 / math.factorial(degree + 1)))
        low_power, high_power = low_power * lower, high_power * upper
    return weights


def spatial(stiff, target, start, values):
    cells = values[0].shape[1]
    columns = jnp.concatenate([stacked(value) for value in values], axis=1)
    target[:, start * cells : (start + len(values)) * cells] = product(stiff[...], columns)


def mixed(rows, source, starts, basis):
    cells = rows(0, 0, 0).shape[1]
    fields = source.shape[1] // cells
    total = [None] * len(starts)
    for direction in range(3):
        for inner in range(fields):
            value = source[
                direction * basis : (direction + 1) * basis, inner * cells : (inner + 1) * cells
            ]
            for i, outer in enumerate(starts):
                term = rows(outer, inner, direction) * value
                total[i] = term if total[i] is None else total[i] + term
    return total


def rows_of(jac):
    return lambda outer, inner, direction: jac[outer, inner, pl.ds(direction, 1), :]


def later_weights_of(clusters, substep):
    goes_on = clusters > 0
    return [jnp.where(goes_on, w, 0.0) for w in taylor_weights(clusters, substep + 1)]


def series(current, rows, stiff, weights, own, first, second, later=None, later_weights=None):
    fields, basis, _ = own.shape
    start = 0
    for size in GROUPS:
        values = [current(start + i) for i in range(size)]
        for i in range(size):
            own[start + i] = values[i] * weights[0]
            if later is not None:
                later[start + i] = values[i] * later_weights[0]
        spatial(stiff, first, start, values)
        start += size
    source, target = first, second
    for degree in range(1, ORDER):
        start = 0
        for size in GROUPS:
            total = mixed(rows, source, range(start, start + size), basis)
            for i in range(size):
                own[start + i] += total[i] * weights[degree]
                if later is not None:
                    later[start + i] += total[i] * later_weights[degree]
            if degree < ORDER - 1:
                spatial(stiff, target, start, total)
            start += size
        source, target = target, source


def split_columns(values):
    high = values.astype(jnp.bfloat16)
    low = (values - high.astype(jnp.float32)).astype(jnp.bfloat16)
    return jnp.concatenate([high, low], axis=1)


def short_series(current, paired, stiff, gather, scatter, later, own, total, first, second):
    fields, basis, cells = own.shape
    pairs = (fields + 1) // 2
    left = lax.broadcasted_iota(jnp.int32, (1, cells), 1) < cells // 2
    weights = [STEP_LENGTH ** (k + 1) / math.factorial(k + 1) for k in range(ORDER)]

    def both(value):
        turned = pltpu.roll(value, cells // 2, 1)
        return [jnp.where(left, value, turned), jnp.where(left, turned, value)]

    rows = jnp.concatenate([current(field) for field in range(fields)], axis=0)
    picked = product(split_columns(rows), gather[...])
    values = [picked[field * basis : (field + 1) * basis] for field in range(fields)]
    for pair in range(pairs):
        other = values[min(2 * pair + 1, fields - 1)]
        total[pair * basis : (pair + 1) * basis, :] = (
            jnp.where(left, values[2 * pair], other) * weights[0]
        )
    for start, size in ((0, 5), (5, 4)):
        spatial(stiff, first, start, values[start : start + size])
    source, target = first, second
    for degree in range(1, ORDER):
        start = 0
        for size in PAIR_GROUPS:
            sums = mixed(rows_of(paired), source, range(start, start + size), basis)
            spread = []
            for i in range(size):
                total[(start + i) * basis : (start + i + 1) * basis, :] += sums[i] * weights[degree]
                if degree < ORDER - 1:
                    spread += both(sums[i])
            if degree < ORDER - 1:
                spatial(stiff, target, 2 * start, spread[: fields - 2 * start])
            start += size
        source, target = target, source
    back = product(split_columns(total[...]), scatter[...])
    for field in range(fields):
        pair, half = divmod(field, 2)
        own[field] = (
            later[field] + back[pair * basis : (pair + 1) * basis, half * cells : (half + 1) * cells]
        )


def pack(own, picks, messages):
    fields, basis, cells = own.shape
    rows = own[...].reshape(fields * basis, cells)
    high = rows.astype(jnp.bfloat16)
    low = (rows - high.astype(jnp.float32)).astype(jnp.bfloat16)
    picked = product(jnp.concatenate([high, low], axis=1), picks[...])
    entries = cells // (fields - 1)
    lane = lax.broadcasted_iota(jnp.int32, (1, cells), 1) // entries
    for exchange, message in enumerate(messages):
        columns = slice(exchange * cells, (exchange + 1) * cells)
        main = picked[0:basis, columns]
        for field in range(1, fields - 1):
            main = jnp.where(lane == field, picked[field * basis : (field + 1) * basis, columns], main)
        message[0:basis, :] = main
        last = (fields - 1) * basis
        rest = picked[last : last + 8, columns]
        for tile in range(1, basis // 8):
            rest = jnp.where(
                lane == tile, picked[last + tile * 8 : last + tile * 8 + 8, columns], rest
            )
        message[basis : basis + 8, :] = rest


def start_kernel(
    stiffness_far, sends_far, clusters_far, coefficients_far, jac_far, *rest
):
    far, rest = rest[:7], rest[7:]
    own, later, message_0, message_1, message_2, message_3, stiff, picks = rest[:8]
    clusters, coefficients, jac, stiffness = rest[8:12]
    near, (first, second, sends, arrived) = rest[12:19], rest[19:]
    fields, basis, cells = own.shape
    pairs = (
        (stiffness_far, stiffness),
        (sends_far, sends),
        (clusters_far, clusters),
        (coefficients_far, coefficients),
        (jac_far, jac),
        *zip(far, near),
    )
    copies = [
        pltpu.make_async_copy(source, target, arrived.at[i])
        for i, (source, target) in enumerate(pairs)
    ]
    for copy in copies:
        copy.start()
    copies[0].wait()
    stiff[...] = widened(-stiffness[...].reshape(3 * basis, basis))
    copies[1].wait()
    entries = sends.shape[1]
    rows = directions()
    places = []
    for row in rows:
        entry_row = sends[pl.ds(row, 1), :]
        places += [entry_row] * (cells // entries)
    place = jnp.concatenate(places, axis=1)
    element = lax.broadcasted_iota(jnp.int32, (cells, place.shape[1]), 0)
    hot = jnp.where(element == place, 1.0, 0.0).astype(jnp.bfloat16)
    picks[0:cells, :] = hot
    picks[cells : 2 * cells, :] = hot
    for copy in copies[2:5]:
        copy.wait()
    weights = taylor_weights(clusters[...], 0)
    series(
        lambda field: coefficients[field], rows_of(jac), stiff, weights, own, first, second,
        later, later_weights_of(clusters[...], 0),
    )
    pack(own, picks, (message_0, message_1, message_2, message_3))
    for copy in copies[5:]:
        copy.wait()


def local_kernel(own, jac, flux_local, matrices, local_hot, volume, local_flux, traces, spatials):
    local_part(
        own, rows_of(jac), flux_local, matrices, local_hot, volume, local_flux, traces, spatials
    )


def local_part(own, rows, flux_local, matrices, local_hot, volume, local_flux, traces, spatial):
    fields, basis, cells = own.shape
    wide = traces.shape[0] // fields
    columns = jnp.concatenate([stacked(own[field]) for field in range(fields)], axis=1)
    spatial[...] = product(matrices[...], columns)
    start = 0
    for size in GROUPS:
        for i, total in enumerate(mixed(rows, spatial, range(start, start + size), basis)):
            volume[start + i] = total
        start += size
    base = 3 * basis
    for face in range(FACES):
        total = [None] * fields
        for inner in range(fields):
            value = spatial[
                base + face * wide : base + (face + 1) * wide, inner * cells : (inner + 1) * cells
            ]
            for outer in range(fields):
                term = flux_local[outer, inner, pl.ds(face, 1), :] * value
                total[outer] = term if total[outer] is None else total[outer] + term
        for outer in range(fields):
            local_flux[face, outer] = total[outer]
    base += FACES * wide
    highs, lows = [], []
    for pair in range(ORIENTS):
        rows = slice(base + pair * wide, base + (pair + 1) * wide)
        values = jnp.concatenate(
            [spatial[rows, field * cells : (field + 1) * cells] for field in range(fields)], axis=0
        )
        high = rounded(values)
        highs.append(high)
        lows.append(values - high)
    left = jnp.concatenate(
        [jnp.concatenate(highs, axis=1), jnp.concatenate(lows, axis=1)], axis=0
    ).astype(jnp.bfloat16)
    both = product(left, local_hot[...])
    half = fields * wide
    traces[...] = both[:half] + both[half:]


def first_local_kernel(
    own, jac, flux_local, stiffness, face_proj, neigh_proj, lifting, slots, orientation, clusters,
    volume, local_flux, traces, matrices, local_hot, halo_hot, halo_pairs, lift,
    paired, gather, scatter,
    spatial, plain, dense,
):
    fields, basis, cells = own.shape
    face_basis = face_proj.shape[0]
    wide = traces.shape[0] // fields
    plain[...] = jnp.zeros_like(plain)
    for direction in range(3):
        plain[direction * basis : (direction + 1) * basis, :] = stiffness[direction].T
    row = 3 * basis
    for face in range(FACES):
        plain[row : row + face_basis, :] = face_proj[:, face, :]
        row += wide
    for pair in range(ORIENTS):
        plain[row : row + face_basis, :] = neigh_proj[pair]
        row += wide
    matrices[...] = widened(plain[...])
    empty = jnp.zeros((wide - face_basis, basis), jnp.float32)
    parts = []
    for face in range(FACES):
        parts += [lifting[:, face, :], empty]
    lift_plain = jnp.concatenate(parts, axis=0).T
    lift_high = rounded(lift_plain)
    lift[...] = jnp.concatenate([lift_high, lift_high, lift_plain - lift_high], axis=1).astype(
        jnp.bfloat16
    )
    slot_row = jnp.concatenate([slots[face : face + 1, :] for face in range(FACES)], axis=1)
    pair_row = jnp.concatenate([orientation[face : face + 1, :] for face in range(FACES)], axis=1)
    element = lax.broadcasted_iota(jnp.int32, (cells, FACES * cells), 0)
    hit = jnp.where(element == slot_row, pair_row, -1)
    for pair in range(ORIENTS):
        local_hot[pair * cells : (pair + 1) * cells, :] = jnp.where(hit == pair, 1.0, 0.0).astype(
            jnp.bfloat16
        )
    entries = cells // (fields - 1)
    rows = directions()
    keys = [cells + row * entries for row in rows]
    entry = lax.broadcasted_iota(jnp.int32, (cells, 1), 0)
    for exchange in range(4):
        key = keys[exchange] + entry % entries
        halo_hot[exchange * cells : (exchange + 1) * cells, :] = jnp.where(
            slot_row == key, 1.0, 0.0
        ).astype(jnp.bfloat16)
    key = jnp.full((cells, 1), -1, jnp.int32)
    for exchange in range(4):
        key = jnp.where(entry // entries == exchange, keys[exchange] + entry % entries, key)
    halo_hot[4 * cells : 5 * cells, :] = jnp.where(slot_row == key, 1.0, 0.0).astype(jnp.bfloat16)
    pair_rows = jnp.broadcast_to(pair_row.astype(jnp.float32), (8, FACES * cells))
    halo_pairs[...] = lax.dot_general(
        pair_rows.astype(jnp.bfloat16),
        halo_hot[...],
        (((1,), (1,)), ((), ())),
        preferred_element_type=jnp.float32,
    )
    compaction(clusters, jac, dense, paired, gather, scatter)
    local_part(
        own, rows_of(jac), flux_local, matrices, local_hot, volume, local_flux, traces, spatial
    )


def compaction(clusters, jac, dense, paired, gather, scatter):
    fields, depth, cells = dense.shape
    half = cells // 2
    short = jnp.where(clusters[...] == 0, 1.0, 0.0)
    before = jnp.where(
        lax.broadcasted_iota(jnp.int32, (cells, cells), 0)
        < lax.broadcasted_iota(jnp.int32, (cells, cells), 1),
        1.0,
        0.0,
    ).astype(jnp.bfloat16)
    rank = product(jnp.broadcast_to(short, (8, cells)).astype(jnp.bfloat16), before)[0:1, :]
    place = jnp.where(short > 0.5, rank, -1.0)
    row = lax.broadcasted_iota(jnp.int32, (cells, cells), 0)
    hot = jnp.where(place == (row % half).astype(jnp.float32), 1.0, 0.0)
    turned = hot.T.astype(jnp.bfloat16)
    gather[0:cells, :] = turned
    gather[cells : 2 * cells, :] = turned
    sides = jnp.concatenate(
        [jnp.where(row < half, hot, 0.0), jnp.where(row < half, 0.0, hot)], axis=1
    ).astype(jnp.bfloat16)
    scatter[0:cells, :] = sides
    scatter[cells : 2 * cells, :] = sides
    for outer in range(fields):
        for inner in range(fields):
            dense[outer, inner * 3 : inner * 3 + 3, :] = jac[outer, inner]
        dense[outer, 3 * fields :, :] = jnp.zeros((depth - 3 * fields, cells), jnp.float32)
    left = lax.broadcasted_iota(jnp.int32, (1, cells), 1) < half
    picked = product(split_columns(dense[...].reshape(fields * depth, cells)), gather[...])
    for pair in range(paired.shape[0]):
        one = picked[2 * pair * depth : (2 * pair + 1) * depth]
        if 2 * pair + 1 < fields:
            two = picked[(2 * pair + 1) * depth : (2 * pair + 2) * depth]
        else:
            two = jnp.zeros_like(one)
        both = jnp.where(left, one, two)
        for inner in range(fields):
            paired[pair, inner] = both[inner * 3 : inner * 3 + 3]


def remote_part(messages, matrices, halo_hot, halo_pairs, traces):
    cells = messages[0].shape[1]
    basis = messages[0].shape[0] - 8
    half = traces.shape[0]
    wide = (matrices.shape[0] - 3 * basis) // (FACES + ORIENTS)
    fields = half // wide
    entries = cells // (fields - 1)
    lane = lax.broadcasted_iota(jnp.int32, (1, cells), 1) // entries
    last = []
    for tile in range(basis // 8):
        total = jnp.zeros((8, cells), jnp.float32)
        for exchange in range(4):
            value = messages[exchange][basis : basis + 8, :]
            shift = ((exchange - tile) * entries) % cells
            if shift:
                value = pltpu.roll(value, shift, 1)
            total = jnp.where(lane == exchange, value, total)
        last.append(total)
    parts = [message[0:basis, :] for message in messages] + [jnp.concatenate(last, axis=0)]
    columns = jnp.concatenate([stacked(part) for part in parts], axis=1)
    base = 3 * basis + FACES * wide
    projected = product(matrices[base:, :], columns)
    pair_row = halo_pairs[0:1, :]
    chosen = projected[0:wide, :]
    for pair in range(1, ORIENTS):
        chosen = jnp.where(
            pair_row == float(pair), projected[pair * wide : (pair + 1) * wide, :], chosen
        )
    high = rounded(chosen)
    low = chosen - high
    left = []
    for part in (high, low):
        for field in range(fields - 1):
            left.append(
                jnp.concatenate(
                    [
                        jnp.where(lane == field, part[:, c * cells : (c + 1) * cells], 0.0)
                        for c in range(4)
                    ],
                    axis=1,
                )
            )
    most = (fields - 1) * wide
    both = product(jnp.concatenate(left, axis=0).astype(jnp.bfloat16), halo_hot[0 : 4 * cells, :])
    tail = jnp.concatenate([high[:, 4 * cells :], low[:, 4 * cells :]], axis=0)
    both_tail = product(tail.astype(jnp.bfloat16), halo_hot[4 * cells :, :])
    return (
        traces[0:most, :] + both[:most] + both[most:],
        traces[most:, :] + both_tail[:wide] + both_tail[wide:],
    )


def change(remote, volume, local_flux, flux_neigh, lift):
    main, tail = remote
    fields, _, cells = volume.shape
    wide = local_flux.shape[2]
    rows = []
    for face in range(FACES):
        total = [local_flux[face, outer] for outer in range(fields)]
        for inner in range(fields):
            source = main[inner * wide : (inner + 1) * wide] if inner < fields - 1 else tail
            value = source[:, face * cells : (face + 1) * cells]
            for outer in range(fields):
                total[outer] = total[outer] + flux_neigh[outer, inner, pl.ds(face, 1), :] * value
        rows.append(jnp.concatenate(total, axis=1))
    flux = jnp.concatenate(rows, axis=0)
    high = rounded(flux)
    right = jnp.concatenate([high, flux - high, high], axis=0).astype(jnp.bfloat16)
    lifted = product(lift[...], right)
    return [volume[p] - lifted[:, p * cells : (p + 1) * cells] for p in range(fields)]


def step_kernel(
    substep,
    coefficients, applied_in, pending_in, jac, stiff, clusters, picks, in_0, in_1, in_2, in_3,
    volume, local_flux, traces, flux_neigh, matrices, halo_hot, halo_pairs, lift, *rest
):
    if substep % 2 == 0:
        (paired, gather, scatter, later, applied, pending, own, *messages), rest = rest[:11], rest[11:]
        total, first, second = rest
    else:
        (applied, pending, own, later, *messages), (first, second) = rest[:8], rest[8:]
    fields, _, cells = volume.shape
    remote = remote_part((in_0, in_1, in_2, in_3), matrices, halo_hot, halo_pairs, traces)
    updates = change(remote, volume, local_flux, flux_neigh, lift)
    _, done = time_phase(clusters[...], substep)
    finished = done > 0.5
    for field in range(fields):
        waiting = updates[field]
        if substep > 0:
            waiting = waiting + pending_in[field]
        passed = jnp.where(finished, waiting, 0.0)
        applied[field] = passed + applied_in[field] if substep > 0 else passed
        pending[field] = jnp.where(finished, 0.0, waiting)
    weights = taylor_weights(clusters[...], substep + 1)

    def current(field):
        return coefficients[field] + applied[field]

    if substep % 2 == 0:
        fits = jnp.sum(jnp.where(clusters[...] == 0, 1.0, 0.0)) <= cells // 2

        @pl.when(fits)
        def _():
            short_series(current, paired, stiff, gather, scatter, later, own, total, first, second)

        @pl.when(jnp.logical_not(fits))
        def _():
            series(current, rows_of(jac), stiff, weights, own, first, second)
    else:
        series(
            current, rows_of(jac), stiff, weights, own, first, second,
            later, later_weights_of(clusters[...], substep + 1),
        )
    pack(own, picks, messages)


def last_kernel(
    applied_in, pending_in,
    in_0, in_1, in_2, in_3,
    volume, local_flux, traces, flux_neigh, matrices, halo_hot, halo_pairs, lift,
    increment,
):
    remote = remote_part((in_0, in_1, in_2, in_3), matrices, halo_hot, halo_pairs, traces)
    updates = change(remote, volume, local_flux, flux_neigh, lift)
    for field in range(volume.shape[0]):
        increment[field] = applied_in[field] + (pending_in[field] + updates[field])


def call(kernel, outs, scratch, flops, *operands, far=False):
    block = pl.BlockSpec(memory_space=pltpu.VMEM)
    source = pl.BlockSpec(memory_space=pltpu.HBM) if far else block
    if far:
        operands = [pltpu.with_memory_space_constraint(x, pltpu.HBM) for x in operands]
    return pl.pallas_call(
        kernel,
        out_shape=outs,
        in_specs=[source] * len(operands),
        out_specs=[block] * len(outs),
        scratch_shapes=scratch,
        compiler_params=pltpu.CompilerParams(vmem_limit_bytes=40 << 20),
        cost_estimate=pl.CostEstimate(flops=flops, bytes_accessed=1 << 20, transcendentals=0),
    )(*operands)


def on_device(
    coefficients, stiffness, jacobians, face_proj, neigh_proj, lifting,
    flux_local, flux_neigh, clusters, face_slots, orientation, send_list, *, doms, subs,
):
    fields, basis, cells = coefficients.shape
    wide = -(-face_proj.shape[1] // 8) * 8
    clusters = clusters.reshape(1, cells)
    jacobians = jnp.transpose(jacobians, (1, 2, 0, 3))
    flux_local = jnp.transpose(flux_local, (1, 2, 0, 3))
    flux_neigh = jnp.transpose(flux_neigh, (1, 2, 0, 3))
    face_proj = jnp.transpose(face_proj, (1, 0, 2))
    lifting = jnp.transpose(lifting, (2, 0, 1))
    exchanges = [
        swaps(doms, subs, axis, phase) for axis in ("sub", "dom") for phase in (0, 1)
    ]

    def f32(*shape):
        return jax.ShapeDtypeStruct(shape, jnp.float32)

    def bf16(*shape):
        return jax.ShapeDtypeStruct(shape, jnp.bfloat16)

    state = f32(fields, basis, cells)
    message = f32(basis + 8, cells)
    depth = 3 * basis + 8
    rows = 3 * basis + (FACES + ORIENTS) * wide
    derived = pltpu.VMEM((3 * basis, fields * cells), jnp.float32)
    faces = FACES * cells

    def exchange(messages):
        return [lax.ppermute(m, AXES, pairs) for m, pairs in zip(messages, exchanges)]

    first = [stiffness, send_list, clusters, coefficients, jacobians]
    later = [flux_local, flux_neigh, face_proj, neigh_proj, lifting, face_slots, orientation]
    near = [clusters, coefficients, jacobians, stiffness, *later]
    own, later, *given = call(
        start_kernel,
        [state] * 2 + [message] * 4 + [bf16(3 * basis, depth), bf16(2 * cells, 4 * cells)]
        + [jax.ShapeDtypeStruct(x.shape, x.dtype) for x in near],
        [
            derived, derived, pltpu.VMEM(send_list.shape, send_list.dtype),
            pltpu.SemaphoreType.DMA((len(first) + len(later),)),
        ],
        1 << 27, *first, *later, far=True,
    )
    messages, (stiff, picks), near = given[:4], given[4:6], given[6:]
    clusters, coefficients, jacobians, stiffness = near[:4]
    flux_local, flux_neigh, face_proj, neigh_proj, lifting, face_slots, orientation = near[4:]
    local_outs = [state, f32(FACES, fields, wide, cells), f32(fields * wide, faces)]
    spatials = pltpu.VMEM((rows, fields * cells), jnp.float32)
    pairs = (fields + 1) // 2
    depth = -(-3 * fields // 8) * 8
    applied = pending = coefficients
    for substep in range(SUBSTEPS):
        received = exchange(messages)
        if substep == 0:
            volume, local_flux, traces, *given = call(
                first_local_kernel,
                local_outs
                + [
                    bf16(rows, stiff.shape[1]), bf16(ORIENTS * cells, faces), bf16(5 * cells, faces),
                    f32(8, 5 * cells), bf16(basis, 3 * FACES * wide),
                    f32(pairs, fields, 3, cells),
                    bf16(2 * cells, cells), bf16(2 * cells, 2 * cells),
                ],
                [
                    spatials, pltpu.VMEM((rows, basis), jnp.float32),
                    pltpu.VMEM((fields, depth, cells), jnp.float32),
                ],
                1 << 27,
                own, jacobians, flux_local, stiffness, face_proj, neigh_proj, lifting,
                face_slots, orientation, clusters,
            )
            matrices, local_hot, halo_hot, halo_pairs, lift, *compact = given
        else:
            volume, local_flux, traces = call(
                local_kernel, local_outs, [spatials], 1 << 27,
                own, jacobians, flux_local, matrices, local_hot,
            )
        rest = (
            *received, volume, local_flux, traces, flux_neigh, matrices, halo_hot, halo_pairs, lift,
        )
        if substep == SUBSTEPS - 1:
            (increment,) = call(last_kernel, [state], [], 1 << 27, applied, pending, *rest)
            return increment
        most = (coefficients, applied, pending, jacobians, stiff, clusters, picks, *rest)
        kernel = functools.partial(step_kernel, substep)
        if substep % 2 == 0:
            sums = pltpu.VMEM((pairs * basis, cells), jnp.float32)
            applied, pending, own, *messages = call(
                kernel, [state] * 3 + [message] * 4, [sums, derived, derived], 1 << 27,
                *most, *compact, later,
            )
        else:
            applied, pending, own, later, *messages = call(
                kernel, [state] * 4 + [message] * 4, [derived, derived], 1 << 27, *most
            )


def solution(mesh):
    split = ("dom", "sub")
    placed = (
        P(None, None, split), P(), P(None, None, None, split), P(), P(), P(),
        P(None, None, None, split), P(None, None, None, split), P(split),
        P(None, split), P(None, split), P(None, split),
    )
    return jax.shard_map(
        functools.partial(on_device, doms=mesh.shape["dom"], subs=mesh.shape["sub"]),
        mesh=mesh,
        in_specs=placed,
        out_specs=P(None, None, split),
        check_vma=False,
    )
```

```python
import functools
import math

import jax
import jax.numpy as jnp
from jax import lax
from jax.experimental import pallas as pl
from jax.experimental.pallas import tpu as pltpu
from jax.sharding import PartitionSpec as P

ORDER = 6
ORIENTS = 12
FACES = 4
SUBSTEPS = 4
STEP_LENGTH = 0.5
GROUPS = (5, 4)
PAIR_GROUPS = (3, 2)
AXES = ("dom", "sub")


def swaps(doms, subs, axis, phase):
    partner = {}
    for dom in range(doms):
        for sub in range(subs):
            place = sub if axis == "sub" else dom
            count = subs if axis == "sub" else doms
            other = place + 1 if (place - phase) % 2 == 0 else place - 1
            if 0 <= other < count:
                there = (dom, other) if axis == "sub" else (other, sub)
                partner[(dom, sub)] = there
    idle = [(d, s) for d in range(doms) for s in range(subs) if (d, s) not in partner]
    for dom, sub in idle:
        for there in ((dom, sub ^ 1), (dom ^ 1, sub)):
            if (dom, sub) not in partner and there in idle and there not in partner:
                partner[(dom, sub)] = there
                partner[there] = (dom, sub)
    return [
        (dom * subs + sub, there[0] * subs + there[1])
        for (dom, sub), there in sorted(partner.items())
    ]


def rounded(values):
    return values.astype(jnp.bfloat16).astype(jnp.float32)


def stacked(values):
    high = rounded(values)
    low = values - high
    pad = jnp.zeros((8, values.shape[1]), jnp.float32)
    return jnp.concatenate([high, low, high, pad], axis=0).astype(jnp.bfloat16)


def widened(weights):
    high = rounded(weights)
    low = weights - high
    pad = jnp.zeros((weights.shape[0], 8), jnp.float32)
    return jnp.concatenate([high, high, low, pad], axis=1).astype(jnp.bfloat16)


def product(left, right):
    return jnp.dot(left, right, preferred_element_type=jnp.float32)


def directions():
    sub_odd = lax.axis_index("sub") % 2
    dom_odd = lax.axis_index("dom") % 2
    return [1 - sub_odd, sub_odd, 3 - dom_odd, 2 + dom_odd]


def time_phase(clusters, substep):
    phases = [substep % 1, substep % 2, substep % 4]
    ends = [True, (substep + 1) % 2 == 0, (substep + 1) % 4 == 0]
    phase = jnp.where(
        clusters == 0, float(phases[0]), jnp.where(clusters == 1, float(phases[1]), float(phases[2]))
    )
    done = jnp.where(
        clusters == 0, float(ends[0]), jnp.where(clusters == 1, float(ends[1]), float(ends[2]))
    )
    return phase, done


def taylor_weights(clusters, substep):
    phase, _ = time_phase(clusters, substep)
    lower = phase * STEP_LENGTH
    upper = lower + STEP_LENGTH
    weights, low_power, high_power = [], lower, upper
    for degree in range(ORDER):
        weights.append((high_power - low_power) * (1.0 / math.factorial(degree + 1)))
        low_power, high_power = low_power * lower, high_power * upper
    return weights


def spatial(stiff, target, start, values):
    cells = values[0].shape[1]
    columns = jnp.concatenate([stacked(value) for value in values], axis=1)
    target[:, start * cells : (start + len(values)) * cells] = product(stiff[...], columns)


def mixed(rows, source, starts, basis):
    cells = rows(0, 0, 0).shape[1]
    fields = source.shape[1] // cells
    total = [None] * len(starts)
    for direction in range(3):
        for inner in range(fields):
            value = source[
                direction * basis : (direction + 1) * basis, inner * cells : (inner + 1) * cells
            ]
            for i, outer in enumerate(starts):
                term = rows(outer, inner, direction) * value
                total[i] = term if total[i] is None else total[i] + term
    return total


def rows_of(jac):
    return lambda outer, inner, direction: jac[outer, inner, pl.ds(direction, 1), :]


def later_weights_of(clusters, substep):
    goes_on = clusters > 0
    return [jnp.where(goes_on, w, 0.0) for w in taylor_weights(clusters, substep + 1)]


def series(current, rows, stiff, weights, own, first, second, later=None, later_weights=None):
    fields, basis, _ = own.shape
    start = 0
    for size in GROUPS:
        values = [current(start + i) for i in range(size)]
        for i in range(size):
            own[start + i] = values[i] * weights[0]
            if later is not None:
                later[start + i] = values[i] * later_weights[0]
        spatial(stiff, first, start, values)
        start += size
    source, target = first, second
    for degree in range(1, ORDER):
        start = 0
        for size in GROUPS:
            total = mixed(rows, source, range(start, start + size), basis)
            for i in range(size):
                own[start + i] += total[i] * weights[degree]
                if later is not None:
                    later[start + i] += total[i] * later_weights[degree]
            if degree < ORDER - 1:
                spatial(stiff, target, start, total)
            start += size
        source, target = target, source


def picked_lanes(values, places):
    return jnp.take_along_axis(
        values, jnp.broadcast_to(places, values.shape), axis=1, mode="promise_in_bounds"
    )


def split_columns(values):
    high = values.astype(jnp.bfloat16)
    low = (values - high.astype(jnp.float32)).astype(jnp.bfloat16)
    return jnp.concatenate([high, low], axis=1)


def short_series(current, paired, stiff, places, scatter, later, own, total, first, second):
    fields, basis, cells = own.shape
    pairs = (fields + 1) // 2
    left = lax.broadcasted_iota(jnp.int32, (1, cells), 1) < cells // 2
    weights = [STEP_LENGTH ** (k + 1) / math.factorial(k + 1) for k in range(ORDER)]

    def both(value):
        turned = pltpu.roll(value, cells // 2, 1)
        return [jnp.where(left, value, turned), jnp.where(left, turned, value)]

    values = [picked_lanes(current(field), places[0:1, :]) for field in range(fields)]
    for pair in range(pairs):
        other = values[min(2 * pair + 1, fields - 1)]
        total[pair * basis : (pair + 1) * basis, :] = (
            jnp.where(left, values[2 * pair], other) * weights[0]
        )
    for start, size in ((0, 5), (5, 4)):
        spatial(stiff, first, start, values[start : start + size])
    source, target = first, second
    for degree in range(1, ORDER):
        start = 0
        for size in PAIR_GROUPS:
            sums = mixed(rows_of(paired), source, range(start, start + size), basis)
            spread = []
            for i in range(size):
                total[(start + i) * basis : (start + i + 1) * basis, :] += sums[i] * weights[degree]
                if degree < ORDER - 1:
                    spread += both(sums[i])
            if degree < ORDER - 1:
                spatial(stiff, target, 2 * start, spread[: fields - 2 * start])
            start += size
        source, target = target, source
    back = product(split_columns(total[...]), scatter[...])
    for field in range(fields):
        pair, half = divmod(field, 2)
        own[field] = (
            later[field] + back[pair * basis : (pair + 1) * basis, half * cells : (half + 1) * cells]
        )


def pack(own, picks, messages):
    fields, basis, cells = own.shape
    rows = own[...].reshape(fields * basis, cells)
    high = rows.astype(jnp.bfloat16)
    low = (rows - high.astype(jnp.float32)).astype(jnp.bfloat16)
    picked = product(jnp.concatenate([high, low], axis=1), picks[...])
    entries = cells // (fields - 1)
    lane = lax.broadcasted_iota(jnp.int32, (1, cells), 1) // entries
    for exchange, message in enumerate(messages):
        columns = slice(exchange * cells, (exchange + 1) * cells)
        main = picked[0:basis, columns]
        for field in range(1, fields - 1):
            main = jnp.where(lane == field, picked[field * basis : (field + 1) * basis, columns], main)
        message[0:basis, :] = main
        last = (fields - 1) * basis
        rest = picked[last : last + 8, columns]
        for tile in range(1, basis // 8):
            rest = jnp.where(
                lane == tile, picked[last + tile * 8 : last + tile * 8 + 8, columns], rest
            )
        message[basis : basis + 8, :] = rest


def start_kernel(
    stiffness_far, sends_far, clusters_far, coefficients_far, jac_far, *rest
):
    far, rest = rest[:7], rest[7:]
    own, later, message_0, message_1, message_2, message_3, stiff, picks = rest[:8]
    clusters, coefficients, jac, stiffness = rest[8:12]
    near, (first, second, sends, arrived) = rest[12:19], rest[19:]
    fields, basis, cells = own.shape
    pairs = (
        (stiffness_far, stiffness),
        (sends_far, sends),
        (clusters_far, clusters),
        (coefficients_far, coefficients),
        (jac_far, jac),
        *zip(far, near),
    )
    copies = [
        pltpu.make_async_copy(source, target, arrived.at[i])
        for i, (source, target) in enumerate(pairs)
    ]
    for copy in copies:
        copy.start()
    copies[0].wait()
    stiff[...] = widened(-stiffness[...].reshape(3 * basis, basis))
    copies[1].wait()
    entries = sends.shape[1]
    rows = directions()
    places = []
    for row in rows:
        entry_row = sends[pl.ds(row, 1), :]
        places += [entry_row] * (cells // entries)
    place = jnp.concatenate(places, axis=1)
    element = lax.broadcasted_iota(jnp.int32, (cells, place.shape[1]), 0)
    hot = jnp.where(element == place, 1.0, 0.0).astype(jnp.bfloat16)
    picks[0:cells, :] = hot
    picks[cells : 2 * cells, :] = hot
    for copy in copies[2:5]:
        copy.wait()
    weights = taylor_weights(clusters[...], 0)
    series(
        lambda field: coefficients[field], rows_of(jac), stiff, weights, own, first, second,
        later, later_weights_of(clusters[...], 0),
    )
    pack(own, picks, (message_0, message_1, message_2, message_3))
    for copy in copies[5:]:
        copy.wait()


def local_kernel(own, jac, flux_local, matrices, local_hot, volume, local_flux, traces, spatials):
    local_part(
        own, rows_of(jac), flux_local, matrices, local_hot, volume, local_flux, traces, spatials
    )


def local_part(own, rows, flux_local, matrices, local_hot, volume, local_flux, traces, spatial):
    fields, basis, cells = own.shape
    wide = traces.shape[0] // fields
    columns = jnp.concatenate([stacked(own[field]) for field in range(fields)], axis=1)
    spatial[...] = product(matrices[...], columns)
    start = 0
    for size in GROUPS:
        for i, total in enumerate(mixed(rows, spatial, range(start, start + size), basis)):
            volume[start + i] = total
        start += size
    base = 3 * basis
    for face in range(FACES):
        total = [None] * fields
        for inner in range(fields):
            value = spatial[
                base + face * wide : base + (face + 1) * wide, inner * cells : (inner + 1) * cells
            ]
            for outer in range(fields):
                term = flux_local[outer, inner, pl.ds(face, 1), :] * value
                total[outer] = term if total[outer] is None else total[outer] + term
        for outer in range(fields):
            local_flux[face, outer] = total[outer]
    base += FACES * wide
    highs, lows = [], []
    for pair in range(ORIENTS):
        rows = slice(base + pair * wide, base + (pair + 1) * wide)
        values = jnp.concatenate(
            [spatial[rows, field * cells : (field + 1) * cells] for field in range(fields)], axis=0
        )
        high = rounded(values)
        highs.append(high)
        lows.append(values - high)
    left = jnp.concatenate(
        [jnp.concatenate(highs, axis=1), jnp.concatenate(lows, axis=1)], axis=0
    ).astype(jnp.bfloat16)
    both = product(left, local_hot[...])
    half = fields * wide
    traces[...] = both[:half] + both[half:]


def first_local_kernel(
    own, jac, flux_local, stiffness, face_proj, neigh_proj, lifting, slots, orientation, clusters,
    volume, local_flux, traces, matrices, local_hot, halo_hot, halo_pairs, lift,
    paired, places, scatter,
    spatial, plain,
):
    fields, basis, cells = own.shape
    face_basis = face_proj.shape[0]
    wide = traces.shape[0] // fields
    plain[...] = jnp.zeros_like(plain)
    for direction in range(3):
        plain[direction * basis : (direction + 1) * basis, :] = stiffness[direction].T
    row = 3 * basis
    for face in range(FACES):
        plain[row : row + face_basis, :] = face_proj[:, face, :]
        row += wide
    for pair in range(ORIENTS):
        plain[row : row + face_basis, :] = neigh_proj[pair]
        row += wide
    matrices[...] = widened(plain[...])
    empty = jnp.zeros((wide - face_basis, basis), jnp.float32)
    parts = []
    for face in range(FACES):
        parts += [lifting[:, face, :], empty]
    lift_plain = jnp.concatenate(parts, axis=0).T
    lift_high = rounded(lift_plain)
    lift[...] = jnp.concatenate([lift_high, lift_high, lift_plain - lift_high], axis=1).astype(
        jnp.bfloat16
    )
    slot_row = jnp.concatenate([slots[face : face + 1, :] for face in range(FACES)], axis=1)
    pair_row = jnp.concatenate([orientation[face : face + 1, :] for face in range(FACES)], axis=1)
    element = lax.broadcasted_iota(jnp.int32, (cells, FACES * cells), 0)
    hit = jnp.where(element == slot_row, pair_row, -1)
    for pair in range(ORIENTS):
        local_hot[pair * cells : (pair + 1) * cells, :] = jnp.where(hit == pair, 1.0, 0.0).astype(
            jnp.bfloat16
        )
    entries = cells // (fields - 1)
    rows = directions()
    keys = [cells + row * entries for row in rows]
    entry = lax.broadcasted_iota(jnp.int32, (cells, 1), 0)
    for exchange in range(4):
        key = keys[exchange] + entry % entries
        halo_hot[exchange * cells : (exchange + 1) * cells, :] = jnp.where(
            slot_row == key, 1.0, 0.0
        ).astype(jnp.bfloat16)
    key = jnp.full((cells, 1), -1, jnp.int32)
    for exchange in range(4):
        key = jnp.where(entry // entries == exchange, keys[exchange] + entry % entries, key)
    halo_hot[4 * cells : 5 * cells, :] = jnp.where(slot_row == key, 1.0, 0.0).astype(jnp.bfloat16)
    pair_rows = jnp.broadcast_to(pair_row.astype(jnp.float32), (8, FACES * cells))
    halo_pairs[...] = lax.dot_general(
        pair_rows.astype(jnp.bfloat16),
        halo_hot[...],
        (((1,), (1,)), ((), ())),
        preferred_element_type=jnp.float32,
    )
    compaction(clusters, jac, paired, places, scatter)
    local_part(
        own, rows_of(jac), flux_local, matrices, local_hot, volume, local_flux, traces, spatial
    )


def compaction(clusters, jac, paired, places, scatter):
    fields = jac.shape[0]
    cells = clusters.shape[1]
    half = cells // 2
    short = jnp.where(clusters[...] == 0, 1.0, 0.0)
    row = lax.broadcasted_iota(jnp.int32, (cells, cells), 0)
    column = lax.broadcasted_iota(jnp.int32, (cells, cells), 1)
    before = jnp.where(row < column, 1.0, 0.0).astype(jnp.bfloat16)
    rank = product(jnp.broadcast_to(short, (8, cells)).astype(jnp.bfloat16), before)[0:1, :]
    rank = jnp.where(short > 0.5, rank, -1.0)
    hot = jnp.where(rank == (row % half).astype(jnp.float32), 1.0, 0.0)
    element = column[0:8, :].astype(jnp.float32).astype(jnp.bfloat16)
    place = lax.dot_general(
        element, hot.astype(jnp.bfloat16), (((1,), (1,)), ((), ())),
        preferred_element_type=jnp.float32,
    ).astype(jnp.int32)
    places[...] = place
    sides = jnp.concatenate(
        [jnp.where(row < half, hot, 0.0), jnp.where(row < half, 0.0, hot)], axis=1
    ).astype(jnp.bfloat16)
    scatter[0:cells, :] = sides
    scatter[cells : 2 * cells, :] = sides
    left = column[0:1, :] < half
    for pair in range(paired.shape[0]):
        for inner in range(fields):
            one = picked_lanes(jac[2 * pair, inner], place[0:1, :])
            if 2 * pair + 1 < fields:
                two = picked_lanes(jac[2 * pair + 1, inner], place[0:1, :])
            else:
                two = jnp.zeros_like(one)
            paired[pair, inner] = jnp.where(left, one, two)


def remote_part(messages, matrices, halo_hot, halo_pairs, traces):
    cells = messages[0].shape[1]
    basis = messages[0].shape[0] - 8
    half = traces.shape[0]
    wide = (matrices.shape[0] - 3 * basis) // (FACES + ORIENTS)
    fields = half // wide
    entries = cells // (fields - 1)
    lane = lax.broadcasted_iota(jnp.int32, (1, cells), 1) // entries
    last = []
    for tile in range(basis // 8):
        total = jnp.zeros((8, cells), jnp.float32)
        for exchange in range(4):
            value = messages[exchange][basis : basis + 8, :]
            shift = ((exchange - tile) * entries) % cells
            if shift:
                value = pltpu.roll(value, shift, 1)
            total = jnp.where(lane == exchange, value, total)
        last.append(total)
    parts = [message[0:basis, :] for message in messages] + [jnp.concatenate(last, axis=0)]
    columns = jnp.concatenate([stacked(part) for part in parts], axis=1)
    base = 3 * basis + FACES * wide
    projected = product(matrices[base:, :], columns)
    pair_row = halo_pairs[0:1, :]
    chosen = projected[0:wide, :]
    for pair in range(1, ORIENTS):
        chosen = jnp.where(
            pair_row == float(pair), projected[pair * wide : (pair + 1) * wide, :], chosen
        )
    high = rounded(chosen)
    low = chosen - high
    left = []
    for part in (high, low):
        for field in range(fields - 1):
            left.append(
                jnp.concatenate(
                    [
                        jnp.where(lane == field, part[:, c * cells : (c + 1) * cells], 0.0)
                        for c in range(4)
                    ],
                    axis=1,
                )
            )
    most = (fields - 1) * wide
    both = product(jnp.concatenate(left, axis=0).astype(jnp.bfloat16), halo_hot[0 : 4 * cells, :])
    tail = jnp.concatenate([high[:, 4 * cells :], low[:, 4 * cells :]], axis=0)
    both_tail = product(tail.astype(jnp.bfloat16), halo_hot[4 * cells :, :])
    return (
        traces[0:most, :] + both[:most] + both[most:],
        traces[most:, :] + both_tail[:wide] + both_tail[wide:],
    )


def change(remote, volume, local_flux, flux_neigh, lift):
    main, tail = remote
    fields, _, cells = volume.shape
    wide = local_flux.shape[2]
    rows = []
    for face in range(FACES):
        total = [local_flux[face, outer] for outer in range(fields)]
        for inner in range(fields):
            source = main[inner * wide : (inner + 1) * wide] if inner < fields - 1 else tail
            value = source[:, face * cells : (face + 1) * cells]
            for outer in range(fields):
                total[outer] = total[outer] + flux_neigh[outer, inner, pl.ds(face, 1), :] * value
        rows.append(jnp.concatenate(total, axis=1))
    flux = jnp.concatenate(rows, axis=0)
    high = rounded(flux)
    right = jnp.concatenate([high, flux - high, high], axis=0).astype(jnp.bfloat16)
    lifted = product(lift[...], right)
    return [volume[p] - lifted[:, p * cells : (p + 1) * cells] for p in range(fields)]


def step_kernel(
    substep,
    coefficients, applied_in, pending_in, jac, stiff, clusters, picks, in_0, in_1, in_2, in_3,
    volume, local_flux, traces, flux_neigh, matrices, halo_hot, halo_pairs, lift, *rest
):
    if substep % 2 == 0:
        (paired, places, scatter, later, applied, pending, own, *messages), rest = rest[:11], rest[11:]
        total, first, second = rest
    else:
        (applied, pending, own, later, *messages), (first, second) = rest[:8], rest[8:]
    fields, _, cells = volume.shape
    if substep % 2 == 0:
        fits = jnp.sum(jnp.where(clusters[...] == 0, 1.0, 0.0)) <= cells // 2
    remote = remote_part((in_0, in_1, in_2, in_3), matrices, halo_hot, halo_pairs, traces)
    updates = change(remote, volume, local_flux, flux_neigh, lift)
    _, done = time_phase(clusters[...], substep)
    finished = done > 0.5
    for field in range(fields):
        waiting = updates[field]
        if substep > 0:
            waiting = waiting + pending_in[field]
        passed = jnp.where(finished, waiting, 0.0)
        applied[field] = passed + applied_in[field] if substep > 0 else passed
        pending[field] = jnp.where(finished, 0.0, waiting)
    weights = taylor_weights(clusters[...], substep + 1)

    def current(field):
        return coefficients[field] + applied[field]

    if substep % 2 == 0:

        @pl.when(fits)
        def _():
            short_series(current, paired, stiff, places, scatter, later, own, total, first, second)

        @pl.when(jnp.logical_not(fits))
        def _():
            series(current, rows_of(jac), stiff, weights, own, first, second)
    else:
        series(
            current, rows_of(jac), stiff, weights, own, first, second,
            later, later_weights_of(clusters[...], substep + 1),
        )
    pack(own, picks, messages)


def last_kernel(
    applied_in, pending_in,
    in_0, in_1, in_2, in_3,
    volume, local_flux, traces, flux_neigh, matrices, halo_hot, halo_pairs, lift,
    increment,
):
    remote = remote_part((in_0, in_1, in_2, in_3), matrices, halo_hot, halo_pairs, traces)
    updates = change(remote, volume, local_flux, flux_neigh, lift)
    for field in range(volume.shape[0]):
        increment[field] = applied_in[field] + (pending_in[field] + updates[field])


def call(kernel, outs, scratch, flops, *operands, far=False):
    block = pl.BlockSpec(memory_space=pltpu.VMEM)
    source = pl.BlockSpec(memory_space=pltpu.HBM) if far else block
    if far:
        operands = [pltpu.with_memory_space_constraint(x, pltpu.HBM) for x in operands]
    return pl.pallas_call(
        kernel,
        out_shape=outs,
        in_specs=[source] * len(operands),
        out_specs=[block] * len(outs),
        scratch_shapes=scratch,
        compiler_params=pltpu.CompilerParams(vmem_limit_bytes=40 << 20),
        cost_estimate=pl.CostEstimate(flops=flops, bytes_accessed=1 << 20, transcendentals=0),
    )(*operands)


def on_device(
    coefficients, stiffness, jacobians, face_proj, neigh_proj, lifting,
    flux_local, flux_neigh, clusters, face_slots, orientation, send_list, *, doms, subs,
):
    fields, basis, cells = coefficients.shape
    wide = -(-face_proj.shape[1] // 8) * 8
    clusters = clusters.reshape(1, cells)
    jacobians = jnp.transpose(jacobians, (1, 2, 0, 3))
    flux_local = jnp.transpose(flux_local, (1, 2, 0, 3))
    flux_neigh = jnp.transpose(flux_neigh, (1, 2, 0, 3))
    face_proj = jnp.transpose(face_proj, (1, 0, 2))
    lifting = jnp.transpose(lifting, (2, 0, 1))
    exchanges = [
        swaps(doms, subs, axis, phase) for axis in ("sub", "dom") for phase in (0, 1)
    ]

    def f32(*shape):
        return jax.ShapeDtypeStruct(shape, jnp.float32)

    def bf16(*shape):
        return jax.ShapeDtypeStruct(shape, jnp.bfloat16)

    state = f32(fields, basis, cells)
    message = f32(basis + 8, cells)
    depth = 3 * basis + 8
    rows = 3 * basis + (FACES + ORIENTS) * wide
    derived = pltpu.VMEM((3 * basis, fields * cells), jnp.float32)
    faces = FACES * cells

    def exchange(messages):
        return [lax.ppermute(m, AXES, pairs) for m, pairs in zip(messages, exchanges)]

    first = [stiffness, send_list, clusters, coefficients, jacobians]
    later = [flux_local, flux_neigh, face_proj, neigh_proj, lifting, face_slots, orientation]
    near = [clusters, coefficients, jacobians, stiffness, *later]
    own, later, *given = call(
        start_kernel,
        [state] * 2 + [message] * 4 + [bf16(3 * basis, depth), bf16(2 * cells, 4 * cells)]
        + [jax.ShapeDtypeStruct(x.shape, x.dtype) for x in near],
        [
            derived, derived, pltpu.VMEM(send_list.shape, send_list.dtype),
            pltpu.SemaphoreType.DMA((len(first) + len(later),)),
        ],
        1 << 27, *first, *later, far=True,
    )
    messages, (stiff, picks), near = given[:4], given[4:6], given[6:]
    clusters, coefficients, jacobians, stiffness = near[:4]
    flux_local, flux_neigh, face_proj, neigh_proj, lifting, face_slots, orientation = near[4:]
    local_outs = [state, f32(FACES, fields, wide, cells), f32(fields * wide, faces)]
    spatials = pltpu.VMEM((rows, fields * cells), jnp.float32)
    pairs = (fields + 1) // 2
    applied = pending = coefficients
    for substep in range(SUBSTEPS):
        received = exchange(messages)
        if substep == 0:
            volume, local_flux, traces, *given = call(
                first_local_kernel,
                local_outs
                + [
                    bf16(rows, stiff.shape[1]), bf16(ORIENTS * cells, faces), bf16(5 * cells, faces),
                    f32(8, 5 * cells), bf16(basis, 3 * FACES * wide),
                    f32(pairs, fields, 3, cells),
                    jax.ShapeDtypeStruct((8, cells), jnp.int32), bf16(2 * cells, 2 * cells),
                ],
                [
                    spatials, pltpu.VMEM((rows, basis), jnp.float32),
                ],
                1 << 27,
                own, jacobians, flux_local, stiffness, face_proj, neigh_proj, lifting,
                face_slots, orientation, clusters,
            )
            matrices, local_hot, halo_hot, halo_pairs, lift, *compact = given
        else:
            volume, local_flux, traces = call(
                local_kernel, local_outs, [spatials], 1 << 27,
                own, jacobians, flux_local, matrices, local_hot,
            )
        rest = (
            *received, volume, local_flux, traces, flux_neigh, matrices, halo_hot, halo_pairs, lift,
        )
        if substep == SUBSTEPS - 1:
            (increment,) = call(last_kernel, [state], [], 1 << 27, applied, pending, *rest)
            return increment
        most = (coefficients, applied, pending, jacobians, stiff, clusters, picks, *rest)
        kernel = functools.partial(step_kernel, substep)
        if substep % 2 == 0:
            sums = pltpu.VMEM((pairs * basis, cells), jnp.float32)
            applied, pending, own, *messages = call(
                kernel, [state] * 3 + [message] * 4, [sums, derived, derived], 1 << 27,
                *most, *compact, later,
            )
        else:
            applied, pending, own, later, *messages = call(
                kernel, [state] * 4 + [message] * 4, [derived, derived], 1 << 27, *most
            )


def solution(mesh):
    split = ("dom", "sub")
    placed = (
        P(None, None, split), P(), P(None, None, None, split), P(), P(), P(),
        P(None, None, None, split), P(None, None, None, split), P(split),
        P(None, split), P(None, split), P(None, split),
    )
    return jax.shard_map(
        functools.partial(on_device, doms=mesh.shape["dom"], subs=mesh.shape["sub"]),
        mesh=mesh,
        in_specs=placed,
        out_specs=P(None, None, split),
        check_vma=False,
    )
```

```python
import functools
import math

import jax
import jax.numpy as jnp
from jax import lax
from jax.experimental import pallas as pl
from jax.experimental.pallas import tpu as pltpu
from jax.sharding import PartitionSpec as P

ORDER = 6
ORIENTS = 12
FACES = 4
SUBSTEPS = 4
STEP_LENGTH = 0.5
GROUPS = (5, 4)
PAIR_GROUPS = (3, 2)
AXES = ("dom", "sub")


def swaps(doms, subs, axis, phase):
    partner = {}
    for dom in range(doms):
        for sub in range(subs):
            place = sub if axis == "sub" else dom
            count = subs if axis == "sub" else doms
            other = place + 1 if (place - phase) % 2 == 0 else place - 1
            if 0 <= other < count:
                there = (dom, other) if axis == "sub" else (other, sub)
                partner[(dom, sub)] = there
    idle = [(d, s) for d in range(doms) for s in range(subs) if (d, s) not in partner]
    for dom, sub in idle:
        for there in ((dom, sub ^ 1), (dom ^ 1, sub)):
            if (dom, sub) not in partner and there in idle and there not in partner:
                partner[(dom, sub)] = there
                partner[there] = (dom, sub)
    return [
        (dom * subs + sub, there[0] * subs + there[1])
        for (dom, sub), there in sorted(partner.items())
    ]


def rounded(values):
    return values.astype(jnp.bfloat16).astype(jnp.float32)


def stacked(values):
    high = rounded(values)
    low = values - high
    pad = jnp.zeros((8, values.shape[1]), jnp.float32)
    return jnp.concatenate([high, low, high, pad], axis=0).astype(jnp.bfloat16)


def widened(weights):
    high = rounded(weights)
    low = weights - high
    pad = jnp.zeros((weights.shape[0], 8), jnp.float32)
    return jnp.concatenate([high, high, low, pad], axis=1).astype(jnp.bfloat16)


def pairs_start(basis, wide):
    return -(-(3 * basis + FACES * wide) // 16) * 16


def product(left, right):
    return jnp.dot(left, right, preferred_element_type=jnp.float32)


def directions():
    sub_odd = lax.axis_index("sub") % 2
    dom_odd = lax.axis_index("dom") % 2
    return [1 - sub_odd, sub_odd, 3 - dom_odd, 2 + dom_odd]


def time_phase(clusters, substep):
    phases = [substep % 1, substep % 2, substep % 4]
    ends = [True, (substep + 1) % 2 == 0, (substep + 1) % 4 == 0]
    phase = jnp.where(
        clusters == 0, float(phases[0]), jnp.where(clusters == 1, float(phases[1]), float(phases[2]))
    )
    done = jnp.where(
        clusters == 0, float(ends[0]), jnp.where(clusters == 1, float(ends[1]), float(ends[2]))
    )
    return phase, done


def taylor_weights(clusters, substep):
    phase, _ = time_phase(clusters, substep)
    lower = phase * STEP_LENGTH
    upper = lower + STEP_LENGTH
    weights, low_power, high_power = [], lower, upper
    for degree in range(ORDER):
        weights.append((high_power - low_power) * (1.0 / math.factorial(degree + 1)))
        low_power, high_power = low_power * lower, high_power * upper
    return weights


def spatial(stiff, target, start, values):
    cells = values[0].shape[1]
    columns = jnp.concatenate([stacked(value) for value in values], axis=1)
    target[:, start * cells : (start + len(values)) * cells] = product(stiff[...], columns)


def mixed(rows, source, starts, basis):
    cells = rows(0, 0, 0).shape[1]
    fields = source.shape[1] // cells
    total = [None] * len(starts)
    for direction in range(3):
        for inner in range(fields):
            value = source[
                direction * basis : (direction + 1) * basis, inner * cells : (inner + 1) * cells
            ]
            for i, outer in enumerate(starts):
                term = rows(outer, inner, direction) * value
                total[i] = term if total[i] is None else total[i] + term
    return total


def rows_of(jac):
    return lambda outer, inner, direction: jac[outer, inner, pl.ds(direction, 1), :]


def later_weights_of(clusters, substep):
    goes_on = clusters > 0
    return [jnp.where(goes_on, w, 0.0) for w in taylor_weights(clusters, substep + 1)]


def series(current, rows, stiff, weights, own, first, second, later=None, later_weights=None):
    fields, basis, _ = own.shape
    start = 0
    for size in GROUPS:
        values = [current(start + i) for i in range(size)]
        for i in range(size):
            own[start + i] = values[i] * weights[0]
            if later is not None:
                later[start + i] = values[i] * later_weights[0]
        spatial(stiff, first, start, values)
        start += size
    source, target = first, second
    for degree in range(1, ORDER):
        start = 0
        for size in GROUPS:
            total = mixed(rows, source, range(start, start + size), basis)
            for i in range(size):
                own[start + i] += total[i] * weights[degree]
                if later is not None:
                    later[start + i] += total[i] * later_weights[degree]
            if degree < ORDER - 1:
                spatial(stiff, target, start, total)
            start += size
        source, target = target, source


def picked_lanes(values, places):
    return jnp.take_along_axis(
        values, jnp.broadcast_to(places, values.shape), axis=1, mode="promise_in_bounds"
    )


def split_columns(values):
    high = values.astype(jnp.bfloat16)
    low = (values - high.astype(jnp.float32)).astype(jnp.bfloat16)
    return jnp.concatenate([high, low], axis=1)


def short_series(current, paired, stiff, places, scatter, later, own, total, first, second):
    fields, basis, cells = own.shape
    pairs = (fields + 1) // 2
    left = lax.broadcasted_iota(jnp.int32, (1, cells), 1) < cells // 2
    weights = [STEP_LENGTH ** (k + 1) / math.factorial(k + 1) for k in range(ORDER)]

    def both(value):
        turned = pltpu.roll(value, cells // 2, 1)
        return [jnp.where(left, value, turned), jnp.where(left, turned, value)]

    values = [picked_lanes(current(field), places[0:1, :]) for field in range(fields)]
    for pair in range(pairs):
        other = values[min(2 * pair + 1, fields - 1)]
        total[pair * basis : (pair + 1) * basis, :] = (
            jnp.where(left, values[2 * pair], other) * weights[0]
        )
    for start, size in ((0, 5), (5, 4)):
        spatial(stiff, first, start, values[start : start + size])
    source, target = first, second
    for degree in range(1, ORDER):
        start = 0
        for size in PAIR_GROUPS:
            sums = mixed(rows_of(paired), source, range(start, start + size), basis)
            spread = []
            for i in range(size):
                total[(start + i) * basis : (start + i + 1) * basis, :] += sums[i] * weights[degree]
                if degree < ORDER - 1:
                    spread += both(sums[i])
            if degree < ORDER - 1:
                spatial(stiff, target, 2 * start, spread[: fields - 2 * start])
            start += size
        source, target = target, source
    back = product(split_columns(total[...]), scatter[...])
    for field in range(fields):
        pair, half = divmod(field, 2)
        own[field] = (
            later[field] + back[pair * basis : (pair + 1) * basis, half * cells : (half + 1) * cells]
        )


def pack(own, picks, messages):
    fields, basis, cells = own.shape
    rows = own[...].reshape(fields * basis, cells)
    high = rows.astype(jnp.bfloat16)
    low = (rows - high.astype(jnp.float32)).astype(jnp.bfloat16)
    picked = product(jnp.concatenate([high, low], axis=1), picks[...])
    entries = cells // (fields - 1)
    lane = lax.broadcasted_iota(jnp.int32, (1, cells), 1) // entries
    for exchange, message in enumerate(messages):
        columns = slice(exchange * cells, (exchange + 1) * cells)
        main = picked[0:basis, columns]
        for field in range(1, fields - 1):
            main = jnp.where(lane == field, picked[field * basis : (field + 1) * basis, columns], main)
        message[0:basis, :] = main
        last = (fields - 1) * basis
        rest = picked[last : last + 8, columns]
        for tile in range(1, basis // 8):
            rest = jnp.where(
                lane == tile, picked[last + tile * 8 : last + tile * 8 + 8, columns], rest
            )
        message[basis : basis + 8, :] = rest


def start_kernel(
    stiffness_far, sends_far, clusters_far, coefficients_far, jac_far, *rest
):
    far, rest = rest[:7], rest[7:]
    own, later, message_0, message_1, message_2, message_3, stiff, picks = rest[:8]
    clusters, coefficients, jac, stiffness = rest[8:12]
    near, (first, second, sends, arrived) = rest[12:19], rest[19:]
    fields, basis, cells = own.shape
    pairs = (
        (stiffness_far, stiffness),
        (sends_far, sends),
        (clusters_far, clusters),
        (coefficients_far, coefficients),
        (jac_far, jac),
        *zip(far, near),
    )
    copies = [
        pltpu.make_async_copy(source, target, arrived.at[i])
        for i, (source, target) in enumerate(pairs)
    ]
    for copy in copies:
        copy.start()
    copies[0].wait()
    stiff[...] = widened(-stiffness[...].reshape(3 * basis, basis))
    copies[1].wait()
    entries = sends.shape[1]
    rows = directions()
    places = []
    for row in rows:
        entry_row = sends[pl.ds(row, 1), :]
        places += [entry_row] * (cells // entries)
    place = jnp.concatenate(places, axis=1)
    element = lax.broadcasted_iota(jnp.int32, (cells, place.shape[1]), 0)
    hot = jnp.where(element == place, 1.0, 0.0).astype(jnp.bfloat16)
    picks[0:cells, :] = hot
    picks[cells : 2 * cells, :] = hot
    for copy in copies[2:5]:
        copy.wait()
    weights = taylor_weights(clusters[...], 0)
    series(
        lambda field: coefficients[field], rows_of(jac), stiff, weights, own, first, second,
        later, later_weights_of(clusters[...], 0),
    )
    pack(own, picks, (message_0, message_1, message_2, message_3))
    for copy in copies[5:]:
        copy.wait()


def local_kernel(own, jac, flux_local, matrices, local_hot, volume, local_flux, traces, spatials):
    local_part(
        own, rows_of(jac), flux_local, matrices, local_hot, volume, local_flux, traces, spatials
    )


def local_part(own, rows, flux_local, matrices, local_hot, volume, local_flux, traces, spatial):
    fields, basis, cells = own.shape
    wide = traces.shape[0] // fields
    columns = jnp.concatenate([stacked(own[field]) for field in range(fields)], axis=1)
    spatial[...] = product(matrices[...], columns)
    start = 0
    for size in GROUPS:
        for i, total in enumerate(mixed(rows, spatial, range(start, start + size), basis)):
            volume[start + i] = total
        start += size
    base = 3 * basis
    for face in range(FACES):
        total = [None] * fields
        for inner in range(fields):
            value = spatial[
                base + face * wide : base + (face + 1) * wide, inner * cells : (inner + 1) * cells
            ]
            for outer in range(fields):
                term = flux_local[outer, inner, pl.ds(face, 1), :] * value
                total[outer] = term if total[outer] is None else total[outer] + term
        for outer in range(fields):
            local_flux[face, outer] = total[outer]
    base = pairs_start(basis, wide)
    highs, lows = [], []
    for pair in range(ORIENTS):
        rows = slice(base + pair * wide, base + (pair + 1) * wide)
        values = jnp.concatenate(
            [spatial[rows, field * cells : (field + 1) * cells] for field in range(fields)], axis=0
        )
        high = rounded(values)
        highs.append(high)
        lows.append(values - high)
    left = jnp.concatenate(
        [jnp.concatenate(highs, axis=1), jnp.concatenate(lows, axis=1)], axis=0
    ).astype(jnp.bfloat16)
    both = product(left, local_hot[...])
    half = fields * wide
    traces[...] = both[:half] + both[half:]


def first_local_kernel(
    own, jac, flux_local, stiffness, face_proj, neigh_proj, lifting, slots, orientation, clusters,
    volume, local_flux, traces, matrices, local_hot, halo_hot, halo_pairs, lift,
    paired, places, scatter,
    spatial, plain,
):
    fields, basis, cells = own.shape
    face_basis = face_proj.shape[0]
    wide = traces.shape[0] // fields
    plain[...] = jnp.zeros_like(plain)
    for direction in range(3):
        plain[direction * basis : (direction + 1) * basis, :] = stiffness[direction].T
    row = 3 * basis
    for face in range(FACES):
        plain[row : row + face_basis, :] = face_proj[:, face, :]
        row += wide
    row = pairs_start(basis, wide)
    for pair in range(ORIENTS):
        plain[row : row + face_basis, :] = neigh_proj[pair]
        row += wide
    matrices[...] = widened(plain[...])
    empty = jnp.zeros((wide - face_basis, basis), jnp.float32)
    parts = []
    for face in range(FACES):
        parts += [lifting[:, face, :], empty]
    lift_plain = jnp.concatenate(parts, axis=0).T
    lift_high = rounded(lift_plain)
    lift[...] = jnp.concatenate([lift_high, lift_high, lift_plain - lift_high], axis=1).astype(
        jnp.bfloat16
    )
    slot_row = jnp.concatenate([slots[face : face + 1, :] for face in range(FACES)], axis=1)
    pair_row = jnp.concatenate([orientation[face : face + 1, :] for face in range(FACES)], axis=1)
    element = lax.broadcasted_iota(jnp.int32, (cells, FACES * cells), 0)
    hit = jnp.where(element == slot_row, pair_row, -1)
    for pair in range(ORIENTS):
        local_hot[pair * cells : (pair + 1) * cells, :] = jnp.where(hit == pair, 1.0, 0.0).astype(
            jnp.bfloat16
        )
    entries = cells // (fields - 1)
    rows = directions()
    keys = [cells + row * entries for row in rows]
    entry = lax.broadcasted_iota(jnp.int32, (cells, 1), 0)
    for exchange in range(4):
        key = keys[exchange] + entry % entries
        halo_hot[exchange * cells : (exchange + 1) * cells, :] = jnp.where(
            slot_row == key, 1.0, 0.0
        ).astype(jnp.bfloat16)
    key = jnp.full((cells, 1), -1, jnp.int32)
    for exchange in range(4):
        key = jnp.where(entry // entries == exchange, keys[exchange] + entry % entries, key)
    halo_hot[4 * cells : 5 * cells, :] = jnp.where(slot_row == key, 1.0, 0.0).astype(jnp.bfloat16)
    pair_rows = jnp.broadcast_to(pair_row.astype(jnp.float32), (8, FACES * cells))
    halo_pairs[...] = lax.dot_general(
        pair_rows.astype(jnp.bfloat16),
        halo_hot[...],
        (((1,), (1,)), ((), ())),
        preferred_element_type=jnp.float32,
    )
    compaction(clusters, jac, paired, places, scatter)
    local_part(
        own, rows_of(jac), flux_local, matrices, local_hot, volume, local_flux, traces, spatial
    )


def compaction(clusters, jac, paired, places, scatter):
    fields = jac.shape[0]
    cells = clusters.shape[1]
    half = cells // 2
    short = jnp.where(clusters[...] == 0, 1.0, 0.0)
    row = lax.broadcasted_iota(jnp.int32, (cells, cells), 0)
    column = lax.broadcasted_iota(jnp.int32, (cells, cells), 1)
    before = jnp.where(row < column, 1.0, 0.0).astype(jnp.bfloat16)
    rank = product(jnp.broadcast_to(short, (8, cells)).astype(jnp.bfloat16), before)[0:1, :]
    rank = jnp.where(short > 0.5, rank, -1.0)
    hot = jnp.where(rank == (row % half).astype(jnp.float32), 1.0, 0.0)
    element = column[0:8, :].astype(jnp.float32).astype(jnp.bfloat16)
    place = lax.dot_general(
        element, hot.astype(jnp.bfloat16), (((1,), (1,)), ((), ())),
        preferred_element_type=jnp.float32,
    ).astype(jnp.int32)
    places[...] = place
    sides = jnp.concatenate(
        [jnp.where(row < half, hot, 0.0), jnp.where(row < half, 0.0, hot)], axis=1
    ).astype(jnp.bfloat16)
    scatter[0:cells, :] = sides
    scatter[cells : 2 * cells, :] = sides
    left = column[0:1, :] < half
    for pair in range(paired.shape[0]):
        for inner in range(fields):
            one = picked_lanes(jac[2 * pair, inner], place[0:1, :])
            if 2 * pair + 1 < fields:
                two = picked_lanes(jac[2 * pair + 1, inner], place[0:1, :])
            else:
                two = jnp.zeros_like(one)
            paired[pair, inner] = jnp.where(left, one, two)


def remote_part(messages, matrices, halo_hot, halo_pairs, traces):
    cells = messages[0].shape[1]
    basis = messages[0].shape[0] - 8
    half = traces.shape[0]
    wide = (matrices.shape[0] - 3 * basis) // (FACES + ORIENTS)
    fields = half // wide
    entries = cells // (fields - 1)
    lane = lax.broadcasted_iota(jnp.int32, (1, cells), 1) // entries
    last = []
    for tile in range(basis // 8):
        total = jnp.zeros((8, cells), jnp.float32)
        for exchange in range(4):
            value = messages[exchange][basis : basis + 8, :]
            shift = ((exchange - tile) * entries) % cells
            if shift:
                value = pltpu.roll(value, shift, 1)
            total = jnp.where(lane == exchange, value, total)
        last.append(total)
    parts = [message[0:basis, :] for message in messages] + [jnp.concatenate(last, axis=0)]
    columns = jnp.concatenate([stacked(part) for part in parts], axis=1)
    projected = product(matrices[pairs_start(basis, wide) :, :], columns)
    pair_row = halo_pairs[0:1, :]
    chosen = projected[0:wide, :]
    for pair in range(1, ORIENTS):
        chosen = jnp.where(
            pair_row == float(pair), projected[pair * wide : (pair + 1) * wide, :], chosen
        )
    high = rounded(chosen)
    low = chosen - high
    left = []
    for part in (high, low):
        for field in range(fields - 1):
            left.append(
                jnp.concatenate(
                    [
                        jnp.where(lane == field, part[:, c * cells : (c + 1) * cells], 0.0)
                        for c in range(4)
                    ],
                    axis=1,
                )
            )
    most = (fields - 1) * wide
    both = product(jnp.concatenate(left, axis=0).astype(jnp.bfloat16), halo_hot[0 : 4 * cells, :])
    tail = jnp.concatenate([high[:, 4 * cells :], low[:, 4 * cells :]], axis=0)
    both_tail = product(tail.astype(jnp.bfloat16), halo_hot[4 * cells :, :])
    return (
        traces[0:most, :] + both[:most] + both[most:],
        traces[most:, :] + both_tail[:wide] + both_tail[wide:],
    )


def change(remote, volume, local_flux, flux_neigh, lift):
    main, tail = remote
    fields, _, cells = volume.shape
    wide = local_flux.shape[2]
    rows = []
    for face in range(FACES):
        total = [local_flux[face, outer] for outer in range(fields)]
        for inner in range(fields):
            source = main[inner * wide : (inner + 1) * wide] if inner < fields - 1 else tail
            value = source[:, face * cells : (face + 1) * cells]
            for outer in range(fields):
                total[outer] = total[outer] + flux_neigh[outer, inner, pl.ds(face, 1), :] * value
        rows.append(jnp.concatenate(total, axis=1))
    flux = jnp.concatenate(rows, axis=0)
    high = rounded(flux)
    right = jnp.concatenate([high, flux - high, high], axis=0).astype(jnp.bfloat16)
    lifted = product(lift[...], right)
    return [volume[p] - lifted[:, p * cells : (p + 1) * cells] for p in range(fields)]


def step_kernel(
    substep,
    coefficients, applied_in, pending_in, jac, stiff, clusters, picks, in_0, in_1, in_2, in_3,
    volume, local_flux, traces, flux_neigh, matrices, halo_hot, halo_pairs, lift, *rest
):
    if substep % 2 == 0:
        (paired, places, scatter, later, applied, pending, own, *messages), rest = rest[:11], rest[11:]
        total, first, second = rest
    else:
        (applied, pending, own, later, *messages), (first, second) = rest[:8], rest[8:]
    fields, _, cells = volume.shape
    if substep % 2 == 0:
        fits = jnp.sum(jnp.where(clusters[...] == 0, 1.0, 0.0)) <= cells // 2
    remote = remote_part((in_0, in_1, in_2, in_3), matrices, halo_hot, halo_pairs, traces)
    updates = change(remote, volume, local_flux, flux_neigh, lift)
    _, done = time_phase(clusters[...], substep)
    finished = done > 0.5
    for field in range(fields):
        waiting = updates[field]
        if substep > 0:
            waiting = waiting + pending_in[field]
        passed = jnp.where(finished, waiting, 0.0)
        applied[field] = passed + applied_in[field] if substep > 0 else passed
        pending[field] = jnp.where(finished, 0.0, waiting)
    weights = taylor_weights(clusters[...], substep + 1)

    def current(field):
        return coefficients[field] + applied[field]

    if substep % 2 == 0:

        @pl.when(fits)
        def _():
            short_series(current, paired, stiff, places, scatter, later, own, total, first, second)

        @pl.when(jnp.logical_not(fits))
        def _():
            series(current, rows_of(jac), stiff, weights, own, first, second)
    else:
        series(
            current, rows_of(jac), stiff, weights, own, first, second,
            later, later_weights_of(clusters[...], substep + 1),
        )
    pack(own, picks, messages)


def last_kernel(
    applied_in, pending_in,
    in_0, in_1, in_2, in_3,
    volume, local_flux, traces, flux_neigh, matrices, halo_hot, halo_pairs, lift,
    increment,
):
    remote = remote_part((in_0, in_1, in_2, in_3), matrices, halo_hot, halo_pairs, traces)
    updates = change(remote, volume, local_flux, flux_neigh, lift)
    for field in range(volume.shape[0]):
        increment[field] = applied_in[field] + (pending_in[field] + updates[field])


def call(kernel, outs, scratch, flops, *operands, far=False):
    block = pl.BlockSpec(memory_space=pltpu.VMEM)
    source = pl.BlockSpec(memory_space=pltpu.HBM) if far else block
    if far:
        operands = [pltpu.with_memory_space_constraint(x, pltpu.HBM) for x in operands]
    return pl.pallas_call(
        kernel,
        out_shape=outs,
        in_specs=[source] * len(operands),
        out_specs=[block] * len(outs),
        scratch_shapes=scratch,
        compiler_params=pltpu.CompilerParams(vmem_limit_bytes=40 << 20),
        cost_estimate=pl.CostEstimate(flops=flops, bytes_accessed=1 << 20, transcendentals=0),
    )(*operands)


def on_device(
    coefficients, stiffness, jacobians, face_proj, neigh_proj, lifting,
    flux_local, flux_neigh, clusters, face_slots, orientation, send_list, *, doms, subs,
):
    fields, basis, cells = coefficients.shape
    wide = -(-face_proj.shape[1] // 8) * 8
    clusters = clusters.reshape(1, cells)
    jacobians = jnp.transpose(jacobians, (1, 2, 0, 3))
    flux_local = jnp.transpose(flux_local, (1, 2, 0, 3))
    flux_neigh = jnp.transpose(flux_neigh, (1, 2, 0, 3))
    face_proj = jnp.transpose(face_proj, (1, 0, 2))
    lifting = jnp.transpose(lifting, (2, 0, 1))
    exchanges = [
        swaps(doms, subs, axis, phase) for axis in ("sub", "dom") for phase in (0, 1)
    ]

    def f32(*shape):
        return jax.ShapeDtypeStruct(shape, jnp.float32)

    def bf16(*shape):
        return jax.ShapeDtypeStruct(shape, jnp.bfloat16)

    state = f32(fields, basis, cells)
    message = f32(basis + 8, cells)
    depth = 3 * basis + 8
    rows = pairs_start(basis, wide) + ORIENTS * wide
    derived = pltpu.VMEM((3 * basis, fields * cells), jnp.float32)
    faces = FACES * cells

    def exchange(messages):
        return [lax.ppermute(m, AXES, pairs) for m, pairs in zip(messages, exchanges)]

    first = [stiffness, send_list, clusters, coefficients, jacobians]
    later = [flux_local, flux_neigh, face_proj, neigh_proj, lifting, face_slots, orientation]
    near = [clusters, coefficients, jacobians, stiffness, *later]
    own, later, *given = call(
        start_kernel,
        [state] * 2 + [message] * 4 + [bf16(3 * basis, depth), bf16(2 * cells, 4 * cells)]
        + [jax.ShapeDtypeStruct(x.shape, x.dtype) for x in near],
        [
            derived, derived, pltpu.VMEM(send_list.shape, send_list.dtype),
            pltpu.SemaphoreType.DMA((len(first) + len(later),)),
        ],
        1 << 27, *first, *later, far=True,
    )
    messages, (stiff, picks), near = given[:4], given[4:6], given[6:]
    clusters, coefficients, jacobians, stiffness = near[:4]
    flux_local, flux_neigh, face_proj, neigh_proj, lifting, face_slots, orientation = near[4:]
    local_outs = [state, f32(FACES, fields, wide, cells), f32(fields * wide, faces)]
    spatials = pltpu.VMEM((rows, fields * cells), jnp.float32)
    pairs = (fields + 1) // 2
    applied = pending = coefficients
    for substep in range(SUBSTEPS):
        received = exchange(messages)
        if substep == 0:
            volume, local_flux, traces, *given = call(
                first_local_kernel,
                local_outs
                + [
                    bf16(rows, stiff.shape[1]), bf16(ORIENTS * cells, faces), bf16(5 * cells, faces),
                    f32(8, 5 * cells), bf16(basis, 3 * FACES * wide),
                    f32(pairs, fields, 3, cells),
                    jax.ShapeDtypeStruct((8, cells), jnp.int32), bf16(2 * cells, 2 * cells),
                ],
                [
                    spatials, pltpu.VMEM((rows, basis), jnp.float32),
                ],
                1 << 27,
                own, jacobians, flux_local, stiffness, face_proj, neigh_proj, lifting,
                face_slots, orientation, clusters,
            )
            matrices, local_hot, halo_hot, halo_pairs, lift, *compact = given
        else:
            volume, local_flux, traces = call(
                local_kernel, local_outs, [spatials], 1 << 27,
                own, jacobians, flux_local, matrices, local_hot,
            )
        rest = (
            *received, volume, local_flux, traces, flux_neigh, matrices, halo_hot, halo_pairs, lift,
        )
        if substep == SUBSTEPS - 1:
            (increment,) = call(last_kernel, [state], [], 1 << 27, applied, pending, *rest)
            return increment
        most = (coefficients, applied, pending, jacobians, stiff, clusters, picks, *rest)
        kernel = functools.partial(step_kernel, substep)
        if substep % 2 == 0:
            sums = pltpu.VMEM((pairs * basis, cells), jnp.float32)
            applied, pending, own, *messages = call(
                kernel, [state] * 3 + [message] * 4, [sums, derived, derived], 1 << 27,
                *most, *compact, later,
            )
        else:
            applied, pending, own, later, *messages = call(
                kernel, [state] * 4 + [message] * 4, [derived, derived], 1 << 27, *most
            )


def solution(mesh):
    split = ("dom", "sub")
    placed = (
        P(None, None, split), P(), P(None, None, None, split), P(), P(), P(),
        P(None, None, None, split), P(None, None, None, split), P(split),
        P(None, split), P(None, split), P(None, split),
    )
    return jax.shard_map(
        functools.partial(on_device, doms=mesh.shape["dom"], subs=mesh.shape["sub"]),
        mesh=mesh,
        in_specs=placed,
        out_specs=P(None, None, split),
        check_vma=False,
    )
```

```python
import functools
import math

import jax
import jax.numpy as jnp
from jax import lax
from jax.experimental import pallas as pl
from jax.experimental.pallas import tpu as pltpu
from jax.sharding import PartitionSpec as P

ORDER = 6
ORIENTS = 12
FACES = 4
SUBSTEPS = 4
STEP_LENGTH = 0.5
GROUPS = (5, 4)
PAIR_GROUPS = (3, 2)
AXES = ("dom", "sub")


def swaps(doms, subs, axis, phase):
    partner = {}
    for dom in range(doms):
        for sub in range(subs):
            place = sub if axis == "sub" else dom
            count = subs if axis == "sub" else doms
            other = place + 1 if (place - phase) % 2 == 0 else place - 1
            if 0 <= other < count:
                there = (dom, other) if axis == "sub" else (other, sub)
                partner[(dom, sub)] = there
    idle = [(d, s) for d in range(doms) for s in range(subs) if (d, s) not in partner]
    for dom, sub in idle:
        for there in ((dom, sub ^ 1), (dom ^ 1, sub)):
            if (dom, sub) not in partner and there in idle and there not in partner:
                partner[(dom, sub)] = there
                partner[there] = (dom, sub)
    return [
        (dom * subs + sub, there[0] * subs + there[1])
        for (dom, sub), there in sorted(partner.items())
    ]


def rounded(values):
    return values.astype(jnp.bfloat16).astype(jnp.float32)


def stacked(values):
    high = rounded(values)
    low = values - high
    pad = jnp.zeros((8, values.shape[1]), jnp.float32)
    return jnp.concatenate([high, low, high, pad], axis=0).astype(jnp.bfloat16)


def widened(weights):
    high = rounded(weights)
    low = weights - high
    pad = jnp.zeros((weights.shape[0], 8), jnp.float32)
    return jnp.concatenate([high, high, low, pad], axis=1).astype(jnp.bfloat16)


def pairs_start(basis, wide):
    return -(-(3 * basis + FACES * wide) // 16) * 16


def product(left, right):
    return jnp.dot(left, right, preferred_element_type=jnp.float32)


def directions():
    sub_odd = lax.axis_index("sub") % 2
    dom_odd = lax.axis_index("dom") % 2
    return [1 - sub_odd, sub_odd, 3 - dom_odd, 2 + dom_odd]


def time_phase(clusters, substep):
    phases = [substep % 1, substep % 2, substep % 4]
    ends = [True, (substep + 1) % 2 == 0, (substep + 1) % 4 == 0]
    phase = jnp.where(
        clusters == 0, float(phases[0]), jnp.where(clusters == 1, float(phases[1]), float(phases[2]))
    )
    done = jnp.where(
        clusters == 0, float(ends[0]), jnp.where(clusters == 1, float(ends[1]), float(ends[2]))
    )
    return phase, done


def taylor_weights(clusters, substep):
    phase, _ = time_phase(clusters, substep)
    lower = phase * STEP_LENGTH
    upper = lower + STEP_LENGTH
    weights, low_power, high_power = [], lower, upper
    for degree in range(ORDER):
        weights.append((high_power - low_power) * (1.0 / math.factorial(degree + 1)))
        low_power, high_power = low_power * lower, high_power * upper
    return weights


def spatial(stiff, target, start, values):
    cells = values[0].shape[1]
    columns = jnp.concatenate([stacked(value) for value in values], axis=1)
    target[:, start * cells : (start + len(values)) * cells] = product(stiff[...], columns)


def mixed(rows, source, starts, basis):
    cells = rows(0, 0, 0).shape[1]
    fields = source.shape[1] // cells
    total = [None] * len(starts)
    for direction in range(3):
        for inner in range(fields):
            value = source[
                direction * basis : (direction + 1) * basis, inner * cells : (inner + 1) * cells
            ]
            for i, outer in enumerate(starts):
                term = rows(outer, inner, direction) * value
                total[i] = term if total[i] is None else total[i] + term
    return total


def rows_of(jac):
    return lambda outer, inner, direction: jac[outer, inner, pl.ds(direction, 1), :]


def later_weights_of(clusters, substep):
    goes_on = clusters > 0
    return [jnp.where(goes_on, w, 0.0) for w in taylor_weights(clusters, substep + 1)]


def series(current, rows, stiff, weights, own, first, second, later=None, later_weights=None):
    fields, basis, _ = own.shape
    start = 0
    for size in GROUPS:
        values = [current(start + i) for i in range(size)]
        for i in range(size):
            own[start + i] = values[i] * weights[0]
            if later is not None:
                later[start + i] = values[i] * later_weights[0]
        spatial(stiff, first, start, values)
        start += size
    source, target = first, second
    for degree in range(1, ORDER):
        start = 0
        for size in GROUPS:
            total = mixed(rows, source, range(start, start + size), basis)
            for i in range(size):
                own[start + i] += total[i] * weights[degree]
                if later is not None:
                    later[start + i] += total[i] * later_weights[degree]
            if degree < ORDER - 1:
                spatial(stiff, target, start, total)
            start += size
        source, target = target, source


def picked_lanes(values, places):
    return jnp.take_along_axis(
        values, jnp.broadcast_to(places, values.shape), axis=1, mode="promise_in_bounds"
    )


def split_columns(values):
    high = values.astype(jnp.bfloat16)
    low = (values - high.astype(jnp.float32)).astype(jnp.bfloat16)
    return jnp.concatenate([high, low], axis=1)


def short_series(current, paired, stiff, places, scatter, later, own, total, first, second):
    fields, basis, cells = own.shape
    pairs = (fields + 1) // 2
    left = lax.broadcasted_iota(jnp.int32, (1, cells), 1) < cells // 2
    weights = [STEP_LENGTH ** (k + 1) / math.factorial(k + 1) for k in range(ORDER)]

    def both(value):
        turned = pltpu.roll(value, cells // 2, 1)
        return [jnp.where(left, value, turned), jnp.where(left, turned, value)]

    values = [picked_lanes(current(field), places[0:1, :]) for field in range(fields)]
    for pair in range(pairs):
        other = values[min(2 * pair + 1, fields - 1)]
        total[pair * basis : (pair + 1) * basis, :] = (
            jnp.where(left, values[2 * pair], other) * weights[0]
        )
    for start, size in ((0, 5), (5, 4)):
        spatial(stiff, first, start, values[start : start + size])
    source, target = first, second
    for degree in range(1, ORDER):
        start = 0
        for size in PAIR_GROUPS:
            sums = mixed(rows_of(paired), source, range(start, start + size), basis)
            spread = []
            for i in range(size):
                total[(start + i) * basis : (start + i + 1) * basis, :] += sums[i] * weights[degree]
                if degree < ORDER - 1:
                    spread += both(sums[i])
            if degree < ORDER - 1:
                spatial(stiff, target, 2 * start, spread[: fields - 2 * start])
            start += size
        source, target = target, source
    back = product(split_columns(total[...]), scatter[...])
    for field in range(fields):
        pair, half = divmod(field, 2)
        own[field] = (
            later[field] + back[pair * basis : (pair + 1) * basis, half * cells : (half + 1) * cells]
        )


def pack(own, picks, messages):
    fields, basis, cells = own.shape
    rows = own[...].reshape(fields * basis, cells)
    high = rows.astype(jnp.bfloat16)
    low = (rows - high.astype(jnp.float32)).astype(jnp.bfloat16)
    picked = product(jnp.concatenate([high, low], axis=1), picks[...])
    entries = cells // (fields - 1)
    lane = lax.broadcasted_iota(jnp.int32, (1, cells), 1) // entries
    for exchange, message in enumerate(messages):
        columns = slice(exchange * cells, (exchange + 1) * cells)
        main = picked[0:basis, columns]
        for field in range(1, fields - 1):
            main = jnp.where(lane == field, picked[field * basis : (field + 1) * basis, columns], main)
        message[0:basis, :] = main
        last = (fields - 1) * basis
        rest = picked[last : last + 8, columns]
        for tile in range(1, basis // 8):
            rest = jnp.where(
                lane == tile, picked[last + tile * 8 : last + tile * 8 + 8, columns], rest
            )
        message[basis : basis + 8, :] = rest


def start_kernel(
    stiffness_far, sends_far, clusters_far, coefficients_far, jac_far, *rest
):
    far, rest = rest[:7], rest[7:]
    own, later, message_0, message_1, message_2, message_3, stiff, picks = rest[:8]
    clusters, coefficients, jac, stiffness = rest[8:12]
    near, (first, second, sends, arrived) = rest[12:19], rest[19:]
    fields, basis, cells = own.shape
    pairs = (
        (stiffness_far, stiffness),
        (sends_far, sends),
        (clusters_far, clusters),
        (coefficients_far, coefficients),
        (jac_far, jac),
        *zip(far, near),
    )
    copies = [
        pltpu.make_async_copy(source, target, arrived.at[i])
        for i, (source, target) in enumerate(pairs)
    ]
    for copy in copies:
        copy.start()
    copies[0].wait()
    stiff[...] = widened(-stiffness[...].reshape(3 * basis, basis))
    copies[1].wait()
    entries = sends.shape[1]
    rows = directions()
    places = []
    for row in rows:
        entry_row = sends[pl.ds(row, 1), :]
        places += [entry_row] * (cells // entries)
    place = jnp.concatenate(places, axis=1)
    element = lax.broadcasted_iota(jnp.int32, (cells, place.shape[1]), 0)
    hot = jnp.where(element == place, 1.0, 0.0).astype(jnp.bfloat16)
    picks[0:cells, :] = hot
    picks[cells : 2 * cells, :] = hot
    for copy in copies[2:5]:
        copy.wait()
    weights = taylor_weights(clusters[...], 0)
    series(
        lambda field: coefficients[field], rows_of(jac), stiff, weights, own, first, second,
        later, later_weights_of(clusters[...], 0),
    )
    pack(own, picks, (message_0, message_1, message_2, message_3))
    for copy in copies[5:]:
        copy.wait()


def local_kernel(own, jac, flux_local, matrices, local_hot, volume, local_flux, traces, spatials):
    local_part(
        own, rows_of(jac), flux_local, matrices, local_hot, volume, local_flux, traces, spatials
    )


def local_part(own, rows, flux_local, matrices, local_hot, volume, local_flux, traces, spatial):
    fields, basis, cells = own.shape
    wide = traces.shape[0] // fields
    columns = jnp.concatenate([stacked(own[field]) for field in range(fields)], axis=1)
    spatial[...] = product(matrices[...], columns)
    start = 0
    for size in GROUPS:
        for i, total in enumerate(mixed(rows, spatial, range(start, start + size), basis)):
            volume[start + i] = total
        start += size
    base = 3 * basis
    for face in range(FACES):
        total = [None] * fields
        for inner in range(fields):
            value = spatial[
                base + face * wide : base + (face + 1) * wide, inner * cells : (inner + 1) * cells
            ]
            for outer in range(fields):
                term = flux_local[outer, inner, pl.ds(face, 1), :] * value
                total[outer] = term if total[outer] is None else total[outer] + term
        for outer in range(fields):
            local_flux[face, outer] = total[outer]
    base = pairs_start(basis, wide)
    highs, lows = [], []
    for pair in range(ORIENTS):
        rows = slice(base + pair * wide, base + (pair + 1) * wide)
        values = jnp.concatenate(
            [spatial[rows, field * cells : (field + 1) * cells] for field in range(fields)], axis=0
        )
        high = rounded(values)
        highs.append(high)
        lows.append(values - high)
    left = jnp.concatenate(
        [jnp.concatenate(highs, axis=1), jnp.concatenate(lows, axis=1)], axis=0
    ).astype(jnp.bfloat16)
    both = product(left, local_hot[...])
    half = fields * wide
    traces[...] = both[:half] + both[half:]


def first_local_kernel(
    own, jac, flux_local, stiffness, face_proj, neigh_proj, lifting, slots, orientation, clusters,
    volume, local_flux, traces, matrices, local_hot, halo_hot, halo_pairs, lift,
    paired, places, scatter,
    spatial, plain,
):
    fields, basis, cells = own.shape
    face_basis = face_proj.shape[0]
    wide = traces.shape[0] // fields
    plain[...] = jnp.zeros_like(plain)
    for direction in range(3):
        plain[direction * basis : (direction + 1) * basis, :] = stiffness[direction].T
    row = 3 * basis
    for face in range(FACES):
        plain[row : row + face_basis, :] = face_proj[:, face, :]
        row += wide
    row = pairs_start(basis, wide)
    for pair in range(ORIENTS):
        plain[row : row + face_basis, :] = neigh_proj[pair]
        row += wide
    matrices[...] = widened(plain[...])
    empty = jnp.zeros((wide - face_basis, basis), jnp.float32)
    parts = []
    for face in range(FACES):
        parts += [lifting[:, face, :], empty]
    lift_plain = jnp.concatenate(parts, axis=0).T
    lift_high = rounded(lift_plain)
    lift[...] = jnp.concatenate([lift_high, lift_high, lift_plain - lift_high], axis=1).astype(
        jnp.bfloat16
    )
    slot_row = jnp.concatenate([slots[face : face + 1, :] for face in range(FACES)], axis=1)
    pair_row = jnp.concatenate([orientation[face : face + 1, :] for face in range(FACES)], axis=1)
    element = lax.broadcasted_iota(jnp.int32, (cells, FACES * cells), 0)
    hit = jnp.where(element == slot_row, pair_row, -1)
    for pair in range(ORIENTS):
        local_hot[pair * cells : (pair + 1) * cells, :] = jnp.where(hit == pair, 1.0, 0.0).astype(
            jnp.bfloat16
        )
    entries = cells // (fields - 1)
    rows = directions()
    keys = [cells + row * entries for row in rows]
    entry = lax.broadcasted_iota(jnp.int32, (cells, 1), 0)
    for exchange in range(4):
        key = keys[exchange] + entry % entries
        halo_hot[exchange * cells : (exchange + 1) * cells, :] = jnp.where(
            slot_row == key, 1.0, 0.0
        ).astype(jnp.bfloat16)
    key = jnp.full((cells, 1), -1, jnp.int32)
    for exchange in range(4):
        key = jnp.where(entry // entries == exchange, keys[exchange] + entry % entries, key)
    halo_hot[4 * cells : 5 * cells, :] = jnp.where(slot_row == key, 1.0, 0.0).astype(jnp.bfloat16)
    pair_rows = jnp.broadcast_to(pair_row.astype(jnp.float32), (8, FACES * cells))
    halo_pairs[...] = lax.dot_general(
        pair_rows.astype(jnp.bfloat16),
        halo_hot[...],
        (((1,), (1,)), ((), ())),
        preferred_element_type=jnp.float32,
    )
    compaction(clusters, jac, paired, places, scatter)
    local_part(
        own, rows_of(jac), flux_local, matrices, local_hot, volume, local_flux, traces, spatial
    )


def compaction(clusters, jac, paired, places, scatter):
    fields = jac.shape[0]
    cells = clusters.shape[1]
    half = cells // 2
    short = jnp.where(clusters[...] == 0, 1.0, 0.0)
    row = lax.broadcasted_iota(jnp.int32, (cells, cells), 0)
    column = lax.broadcasted_iota(jnp.int32, (cells, cells), 1)
    before = jnp.where(row < column, 1.0, 0.0).astype(jnp.bfloat16)
    rank = product(jnp.broadcast_to(short, (8, cells)).astype(jnp.bfloat16), before)[0:1, :]
    rank = jnp.where(short > 0.5, rank, -1.0)
    hot = jnp.where(rank == (row % half).astype(jnp.float32), 1.0, 0.0)
    element = column[0:8, :].astype(jnp.float32).astype(jnp.bfloat16)
    place = lax.dot_general(
        element, hot.astype(jnp.bfloat16), (((1,), (1,)), ((), ())),
        preferred_element_type=jnp.float32,
    ).astype(jnp.int32)
    places[...] = place
    sides = jnp.concatenate(
        [jnp.where(row < half, hot, 0.0), jnp.where(row < half, 0.0, hot)], axis=1
    ).astype(jnp.bfloat16)
    scatter[0:cells, :] = sides
    scatter[cells : 2 * cells, :] = sides
    left = column[0:1, :] < half
    for pair in range(paired.shape[0]):
        for inner in range(fields):
            one = picked_lanes(jac[2 * pair, inner], place[0:1, :])
            if 2 * pair + 1 < fields:
                two = picked_lanes(jac[2 * pair + 1, inner], place[0:1, :])
            else:
                two = jnp.zeros_like(one)
            paired[pair, inner] = jnp.where(left, one, two)


def remote_part(messages, matrices, halo_hot, halo_pairs, traces):
    cells = messages[0].shape[1]
    basis = messages[0].shape[0] - 8
    half = traces.shape[0]
    wide = (matrices.shape[0] - 3 * basis) // (FACES + ORIENTS)
    fields = half // wide
    entries = cells // (fields - 1)
    lane = lax.broadcasted_iota(jnp.int32, (1, cells), 1) // entries
    last = []
    for tile in range(basis // 8):
        total = jnp.zeros((8, cells), jnp.float32)
        for exchange in range(4):
            value = messages[exchange][basis : basis + 8, :]
            shift = ((exchange - tile) * entries) % cells
            if shift:
                value = pltpu.roll(value, shift, 1)
            total = jnp.where(lane == exchange, value, total)
        last.append(total)
    parts = [message[0:basis, :] for message in messages] + [jnp.concatenate(last, axis=0)]
    columns = jnp.concatenate([stacked(part) for part in parts], axis=1)
    projected = product(matrices[pairs_start(basis, wide) :, :], columns)
    pair_row = halo_pairs[0:1, :]
    chosen = projected[0:wide, :]
    for pair in range(1, ORIENTS):
        chosen = jnp.where(
            pair_row == float(pair), projected[pair * wide : (pair + 1) * wide, :], chosen
        )
    high = rounded(chosen)
    low = chosen - high
    left = []
    for part in (high, low):
        for field in range(fields - 1):
            left.append(
                jnp.concatenate(
                    [
                        jnp.where(lane == field, part[:, c * cells : (c + 1) * cells], 0.0)
                        for c in range(4)
                    ],
                    axis=1,
                )
            )
    most = (fields - 1) * wide
    both = product(jnp.concatenate(left, axis=0).astype(jnp.bfloat16), halo_hot[0 : 4 * cells, :])
    tail = jnp.concatenate([high[:, 4 * cells :], low[:, 4 * cells :]], axis=0)
    both_tail = product(tail.astype(jnp.bfloat16), halo_hot[4 * cells :, :])
    return (
        traces[0:most, :] + both[:most] + both[most:],
        traces[most:, :] + both_tail[:wide] + both_tail[wide:],
    )


def change(remote, volume, local_flux, flux_neigh, lift):
    main, tail = remote
    fields, _, cells = volume.shape
    wide = local_flux.shape[2]
    rows = []
    for face in range(FACES):
        total = [local_flux[face, outer] for outer in range(fields)]
        for inner in range(fields):
            source = main[inner * wide : (inner + 1) * wide] if inner < fields - 1 else tail
            value = source[:, face * cells : (face + 1) * cells]
            for outer in range(fields):
                total[outer] = total[outer] + flux_neigh[outer, inner, pl.ds(face, 1), :] * value
        rows.append(jnp.concatenate(total, axis=1))
    flux = jnp.concatenate(rows, axis=0)
    high = rounded(flux)
    right = jnp.concatenate([high, flux - high, high], axis=0).astype(jnp.bfloat16)
    lifted = product(lift[...], right)
    return [volume[p] - lifted[:, p * cells : (p + 1) * cells] for p in range(fields)]


def step_kernel(
    substep,
    coefficients, applied_in, pending_in, jac, stiff, clusters, picks, in_0, in_1, in_2, in_3,
    volume, local_flux, traces, flux_neigh, matrices, halo_hot, halo_pairs, lift, *rest
):
    if substep % 2 == 0:
        (paired, places, scatter, later, applied, pending, own, *messages), rest = rest[:11], rest[11:]
        total, first, second = rest
    else:
        (applied, pending, own, later, *messages), (first, second) = rest[:8], rest[8:]
    fields, _, cells = volume.shape
    if substep % 2 == 0:
        fits = jnp.sum(jnp.where(clusters[...] == 0, 1.0, 0.0)) <= cells // 2
    else:
        weights = taylor_weights(clusters[...], substep + 1)
        next_weights = later_weights_of(clusters[...], substep + 1)
    _, done = time_phase(clusters[...], substep)
    finished = done > 0.5
    remote = remote_part((in_0, in_1, in_2, in_3), matrices, halo_hot, halo_pairs, traces)
    updates = change(remote, volume, local_flux, flux_neigh, lift)
    for field in range(fields):
        waiting = updates[field]
        if substep > 0:
            waiting = waiting + pending_in[field]
        passed = jnp.where(finished, waiting, 0.0)
        applied[field] = passed + applied_in[field] if substep > 0 else passed
        pending[field] = jnp.where(finished, 0.0, waiting)
    def current(field):
        return coefficients[field] + applied[field]

    if substep % 2 == 0:

        @pl.when(fits)
        def _():
            short_series(current, paired, stiff, places, scatter, later, own, total, first, second)

        @pl.when(jnp.logical_not(fits))
        def _():
            weights = taylor_weights(clusters[...], substep + 1)
            series(current, rows_of(jac), stiff, weights, own, first, second)
    else:
        series(
            current, rows_of(jac), stiff, weights, own, first, second,
            later, next_weights,
        )
    pack(own, picks, messages)


def last_kernel(
    applied_in, pending_in,
    in_0, in_1, in_2, in_3,
    volume, local_flux, traces, flux_neigh, matrices, halo_hot, halo_pairs, lift,
    increment,
):
    remote = remote_part((in_0, in_1, in_2, in_3), matrices, halo_hot, halo_pairs, traces)
    updates = change(remote, volume, local_flux, flux_neigh, lift)
    for field in range(volume.shape[0]):
        increment[field] = applied_in[field] + (pending_in[field] + updates[field])


def call(kernel, outs, scratch, flops, *operands, far=False):
    block = pl.BlockSpec(memory_space=pltpu.VMEM)
    source = pl.BlockSpec(memory_space=pltpu.HBM) if far else block
    if far:
        operands = [pltpu.with_memory_space_constraint(x, pltpu.HBM) for x in operands]
    return pl.pallas_call(
        kernel,
        out_shape=outs,
        in_specs=[source] * len(operands),
        out_specs=[block] * len(outs),
        scratch_shapes=scratch,
        compiler_params=pltpu.CompilerParams(vmem_limit_bytes=40 << 20),
        cost_estimate=pl.CostEstimate(flops=flops, bytes_accessed=1 << 20, transcendentals=0),
    )(*operands)


def on_device(
    coefficients, stiffness, jacobians, face_proj, neigh_proj, lifting,
    flux_local, flux_neigh, clusters, face_slots, orientation, send_list, *, doms, subs,
):
    fields, basis, cells = coefficients.shape
    wide = -(-face_proj.shape[1] // 8) * 8
    clusters = clusters.reshape(1, cells)
    jacobians = jnp.transpose(jacobians, (1, 2, 0, 3))
    flux_local = jnp.transpose(flux_local, (1, 2, 0, 3))
    flux_neigh = jnp.transpose(flux_neigh, (1, 2, 0, 3))
    face_proj = jnp.transpose(face_proj, (1, 0, 2))
    lifting = jnp.transpose(lifting, (2, 0, 1))
    exchanges = [
        swaps(doms, subs, axis, phase) for axis in ("sub", "dom") for phase in (0, 1)
    ]

    def f32(*shape):
        return jax.ShapeDtypeStruct(shape, jnp.float32)

    def bf16(*shape):
        return jax.ShapeDtypeStruct(shape, jnp.bfloat16)

    state = f32(fields, basis, cells)
    message = f32(basis + 8, cells)
    depth = 3 * basis + 8
    rows = pairs_start(basis, wide) + ORIENTS * wide
    derived = pltpu.VMEM((3 * basis, fields * cells), jnp.float32)
    faces = FACES * cells

    def exchange(messages):
        return [lax.ppermute(m, AXES, pairs) for m, pairs in zip(messages, exchanges)]

    first = [stiffness, send_list, clusters, coefficients, jacobians]
    later = [flux_local, flux_neigh, face_proj, neigh_proj, lifting, face_slots, orientation]
    near = [clusters, coefficients, jacobians, stiffness, *later]
    own, later, *given = call(
        start_kernel,
        [state] * 2 + [message] * 4 + [bf16(3 * basis, depth), bf16(2 * cells, 4 * cells)]
        + [jax.ShapeDtypeStruct(x.shape, x.dtype) for x in near],
        [
            derived, derived, pltpu.VMEM(send_list.shape, send_list.dtype),
            pltpu.SemaphoreType.DMA((len(first) + len(later),)),
        ],
        1 << 27, *first, *later, far=True,
    )
    messages, (stiff, picks), near = given[:4], given[4:6], given[6:]
    clusters, coefficients, jacobians, stiffness = near[:4]
    flux_local, flux_neigh, face_proj, neigh_proj, lifting, face_slots, orientation = near[4:]
    local_outs = [state, f32(FACES, fields, wide, cells), f32(fields * wide, faces)]
    spatials = pltpu.VMEM((rows, fields * cells), jnp.float32)
    pairs = (fields + 1) // 2
    applied = pending = coefficients
    for substep in range(SUBSTEPS):
        received = exchange(messages)
        if substep == 0:
            volume, local_flux, traces, *given = call(
                first_local_kernel,
                local_outs
                + [
                    bf16(rows, stiff.shape[1]), bf16(ORIENTS * cells, faces), bf16(5 * cells, faces),
                    f32(8, 5 * cells), bf16(basis, 3 * FACES * wide),
                    f32(pairs, fields, 3, cells),
                    jax.ShapeDtypeStruct((8, cells), jnp.int32), bf16(2 * cells, 2 * cells),
                ],
                [
                    spatials, pltpu.VMEM((rows, basis), jnp.float32),
                ],
                1 << 27,
                own, jacobians, flux_local, stiffness, face_proj, neigh_proj, lifting,
                face_slots, orientation, clusters,
            )
            matrices, local_hot, halo_hot, halo_pairs, lift, *compact = given
        else:
            volume, local_flux, traces = call(
                local_kernel, local_outs, [spatials], 1 << 27,
                own, jacobians, flux_local, matrices, local_hot,
            )
        rest = (
            *received, volume, local_flux, traces, flux_neigh, matrices, halo_hot, halo_pairs, lift,
        )
        if substep == SUBSTEPS - 1:
            (increment,) = call(last_kernel, [state], [], 1 << 27, applied, pending, *rest)
            return increment
        most = (coefficients, applied, pending, jacobians, stiff, clusters, picks, *rest)
        kernel = functools.partial(step_kernel, substep)
        if substep % 2 == 0:
            sums = pltpu.VMEM((pairs * basis, cells), jnp.float32)
            applied, pending, own, *messages = call(
                kernel, [state] * 3 + [message] * 4, [sums, derived, derived], 1 << 27,
                *most, *compact, later,
            )
        else:
            applied, pending, own, later, *messages = call(
                kernel, [state] * 4 + [message] * 4, [derived, derived], 1 << 27, *most
            )


def solution(mesh):
    split = ("dom", "sub")
    placed = (
        P(None, None, split), P(), P(None, None, None, split), P(), P(), P(),
        P(None, None, None, split), P(None, None, None, split), P(split),
        P(None, split), P(None, split), P(None, split),
    )
    return jax.shard_map(
        functools.partial(on_device, doms=mesh.shape["dom"], subs=mesh.shape["sub"]),
        mesh=mesh,
        in_specs=placed,
        out_specs=P(None, None, split),
        check_vma=False,
    )
```
